256 devices in a mesh: lon: 64 (over x, y_lo, z), lat: 4 (over y_hi, core).
Axes of the slice: x: 4, y: 4 (y_hi: 2, y_lo: 2; y = y_hi * 2 + y_lo), z: 8, core: 2. Of those that a mesh axis runs over, the one named last changes fastest.
Arguments:
- features: bfloat16 [4, 24, 768, 512], P(None, 'lat', 'lon'), may hold values from -6 to 6
- norm_gain: float32 [512], replicated, may hold values from 0.1 to 1.9
- qkv_weight: bfloat16 [512, 1536], replicated, may hold values from -0.25 to 0.25
- proj_weight: bfloat16 [512, 512], replicated, may hold values from -0.25 to 0.25
- bias_table: float32 [8, 759], replicated, may hold values from -4 to 4
- merge_gain: float32 [2048], replicated, may hold values from 0.1 to 1.9
- merge_weight: bfloat16 [2048, 1024], replicated, may hold values from -0.125 to 0.125
- merged_cot: bfloat16 [4, 12, 384, 1024], P(None, 'lat', 'lon'), may hold values from -6 to 6
Outputs:
- merged: bfloat16 [4, 12, 384, 1024], P(None, 'lat', 'lon')
- features_grad: bfloat16 [4, 24, 768, 512], P(None, 'lat', 'lon')
- qkv_grad: float32 [512, 1536], P('lon', 'lat')
- proj_grad: float32 [512, 512], P('lon', 'lat')
- merge_grad: float32 [2048, 1024], P('lon', 'lat')
- norm_gain_grad: float32 [512], replicated
- merge_gain_grad: float32 [2048], replicated
- bias_grad: float32 [8, 759], replicated
The draws below stay inside these ranges and needn't reach their ends.
All inputs are finite; a program needn't handle non-finite values.
Results may differ from the reference program's by a relative error of at most 0.025.
Values may be sent and summed in bfloat16 or wider, within the bound.
No kernel may reach another device: no remote copies, remote signals or barrier semaphores. Data moves between devices by JAX's collectives and lax.ppermute only.
A program may use at most 128 MiB of HBM per device.

```python
import jax
import jax.numpy as jnp
from jax import lax

D = 512
HEADS = 8
LEV = 4
W_LEV = 2
W_LAT = 6
W_LON = 12
LAT_DEV = 6
LON_DEV = 12
BIAS = 759
LAT = 24
LON = 768
N_LON = 64
N_LAT = 4


def block_scale(stream_key, extent, split, least, high):
    loudness, own = 1.0, jax.random.fold_in(stream_key, 6)
    for position, shards_of in split:
        draws = jnp.exp(jax.random.uniform(jax.random.fold_in(own, position), (shards_of,), jnp.float32, least / len(split), high / len(split)))
        loudness = loudness * jnp.repeat(draws, extent[position] // shards_of).reshape([-1 if axis == position else 1 for axis in range(len(extent))])
    return loudness


def normal_values(stream_key, extent, scale, reach, pieces=(), held_as=jnp.bfloat16):
    array = jax.random.normal(stream_key, extent, jnp.float32) * scale
    if len(pieces) > 0:
        array = block_scale(stream_key, extent, pieces, -0.22, 0.18) * array
    return jnp.clip(array, min=-reach, max=reach).astype(held_as)


def setup_inputs(seed: int = 0) -> dict:
    keys = jax.random.split(jax.random.key(seed), 9)
    features = normal_values(keys[0], (LEV, LAT, LON, D), 1.0, 6.0, ((1, 4), (2, 64)))
    norm_gain = jnp.clip(1.0 + 0.18 * jax.random.normal(keys[1], (D,), jnp.float32), 0.1, 1.9)
    qkv_weight = normal_values(keys[2], (D, 3 * D), D ** -0.5, 0.25)
    proj_weight = normal_values(keys[3], (D, D), D ** -0.5, 0.25)
    bias_table = normal_values(keys[4], (HEADS, BIAS), 1.0, 4.0, (), jnp.float32)
    merge_gain = jnp.clip(1.0 + 0.18 * jax.random.normal(keys[5], (4 * D,), jnp.float32), 0.1, 1.9)
    merge_weight = normal_values(keys[6], (4 * D, 2 * D), (4 * D) ** -0.5, 0.125)
    merged_cot = normal_values(keys[7], (LEV, LAT // 2, LON // 2, 2 * D), 1.0, 6.0, ((1, 4), (2, 64)))
    return {"features": features, "norm_gain": norm_gain, "qkv_weight": qkv_weight, "proj_weight": proj_weight, "bias_table": bias_table, "merge_gain": merge_gain, "merge_weight": merge_weight, "merged_cot": merged_cot}


EPSILON = 1e-05
MASKED = -1000000000.0

def normalize(values, gain):
    floats = values.astype(jnp.float32)
    center = floats - lax.optimization_barrier(jnp.mean(floats, axis=-1, keepdims=True))
    spread = lax.optimization_barrier(jnp.mean(center * center, axis=-1, keepdims=True))
    return (center * lax.rsqrt(spread + EPSILON) * gain).astype(jnp.bfloat16)

def relative_bias(table):
    window = W_LEV * W_LAT * W_LON
    places = jnp.arange(window, dtype=jnp.int32)
    level_pos = places // (W_LAT * W_LON)
    north_pos = places // W_LON % W_LAT
    east_pos = places % W_LON
    index = (level_pos[:, None] - level_pos[None, :] + W_LEV - 1) * (2 * W_LAT - 1)
    index = (index + north_pos[:, None] - north_pos[None, :] + W_LAT - 1) * (2 * W_LON - 1)
    index = index + east_pos[:, None] - east_pos[None, :] + W_LON - 1
    return jnp.take(table, index, axis=1)

def to_windows(field):
    levels, height, across, width = field.shape
    parted = field.reshape(levels // W_LEV, W_LEV, height // W_LAT, W_LAT, across // W_LON, W_LON, width)
    return parted.transpose(0, 2, 4, 1, 3, 5, 6).reshape(-1, W_LEV * W_LAT * W_LON, width)

def from_windows(windows, levels, height, across):
    width = windows.shape[-1]
    parted = windows.reshape(levels // W_LEV, height // W_LAT, across // W_LON, W_LEV, W_LAT, W_LON, width)
    return parted.transpose(0, 3, 1, 4, 2, 5, 6).reshape(levels, height, across, width)

def region_ids(levels, height, across, lat_start, lat_total):
    level_idx = jnp.arange(levels, dtype=jnp.int32)
    level_reg = (level_idx >= levels - W_LEV).astype(jnp.int32) + (level_idx >= levels - W_LEV // 2).astype(jnp.int32)
    north_idx = lat_start + jnp.arange(height, dtype=jnp.int32)
    north_reg = (north_idx >= lat_total - W_LAT).astype(jnp.int32) + (north_idx >= lat_total - W_LAT // 2).astype(jnp.int32)
    labels = level_reg[:, None, None] * 3 + north_reg[None, :, None] + jnp.zeros((1, 1, across), jnp.int32)
    return to_windows(labels[..., None])[..., 0]

def window_attention(shifted, qkv_weight, proj_weight, table, lat_start, lat_total):
    levels, height, across, width = shifted.shape
    windows = to_windows(shifted)
    count, window = (windows.shape[0], windows.shape[1])
    head_dim = width // HEADS
    packed = jnp.dot(windows.reshape(-1, width), qkv_weight, preferred_element_type=jnp.float32)
    packed = packed.astype(jnp.bfloat16).reshape(count, window, 3, HEADS, head_dim)
    query = packed[:, :, 0].astype(jnp.float32)
    key_part = packed[:, :, 1].astype(jnp.float32)
    value_part = packed[:, :, 2].astype(jnp.float32)
    scores = jnp.einsum('nqhd,nkhd->nhqk', query, key_part, precision=lax.Precision.HIGHEST) * head_dim ** (-0.5)
    labels = region_ids(levels, height, across, lat_start, lat_total)
    masking = jnp.where(labels[:, :, None] == labels[:, None, :], 0.0, MASKED).astype(jnp.float32)
    scores = scores + relative_bias(table)[None] + masking[:, None]
    weights = jax.nn.softmax(scores, axis=-1).astype(jnp.bfloat16)
    mixed = jnp.einsum('nhqk,nkhd->nqhd', weights.astype(jnp.float32), value_part, precision=lax.Precision.HIGHEST)
    mixed = mixed.astype(jnp.bfloat16).reshape(count * window, width)
    output = jnp.dot(mixed, proj_weight, preferred_element_type=jnp.float32).astype(jnp.bfloat16)
    return from_windows(output.reshape(count, window, width), levels, height, across)

def merge_patches(values, attended, gain, merge_weight):
    summed = (values.astype(jnp.float32) + attended.astype(jnp.float32)).astype(jnp.bfloat16)
    summed = lax.optimization_barrier(summed)
    levels, height, across, width = summed.shape
    stacked = summed.reshape(levels, height // 2, 2, across // 2, 2, width).transpose(0, 1, 3, 4, 2, 5)
    stacked = stacked.reshape(levels, height // 2, across // 2, 4 * width)
    normed = normalize(stacked, gain)
    return jnp.dot(normed, merge_weight, preferred_element_type=jnp.float32).astype(jnp.bfloat16)

def to_blocks(field, height, across):
    levels, width = (field.shape[0], field.shape[-1])
    parted = field.reshape(levels, N_LAT, height, N_LON, across, width)
    return parted.transpose(1, 3, 0, 2, 4, 5).reshape(N_LAT * N_LON, levels, height, across, width)

def from_blocks(blocks):
    levels, height, across, width = blocks.shape[1:]
    parted = blocks.reshape(N_LAT, N_LON, levels, height, across, width)
    return parted.transpose(2, 0, 3, 1, 4, 5).reshape(levels, N_LAT * height, N_LON * across, width)

def reference(features, norm_gain, qkv_weight, proj_weight, bias_table, merge_gain, merge_weight, merged_cot):
    lat_total = LAT
    ahead = (-(W_LEV // 2), -(W_LAT // 2), -(W_LON // 2))
    behind = (W_LEV // 2, W_LAT // 2, W_LON // 2)
    normed, pull_norm = jax.vjp(normalize, features, norm_gain)
    shifted = jnp.roll(normed, ahead, axis=(0, 1, 2))
    starts = jnp.arange(N_LAT * N_LON, dtype=jnp.int32) // N_LON * LAT_DEV

    def attend_block(carry, item):
        block, start = item
        return (carry, window_attention(block, qkv_weight, proj_weight, bias_table, start, lat_total))
    shifted_blocks = to_blocks(shifted, LAT_DEV, LON_DEV)
    _, attn_blocks = lax.scan(attend_block, jnp.zeros((), jnp.float32), (shifted_blocks, starts))
    attended = jnp.roll(from_blocks(attn_blocks), behind, axis=(0, 1, 2))

    def merge_block(carry, item):
        value_block, attn_block, cot_block = item
        merged_block, pull = jax.vjp(merge_patches, value_block, attn_block, merge_gain, merge_weight)
        res_part, attn_part, gain_part, weight_part = pull(cot_block)
        return ((carry[0] + gain_part, carry[1] + weight_part.astype(jnp.float32)), (merged_block, res_part, attn_part))
    merge_init = (jnp.zeros(merge_gain.shape, jnp.float32), jnp.zeros(merge_weight.shape, jnp.float32))
    merge_items = (to_blocks(features, LAT_DEV, LON_DEV), to_blocks(attended, LAT_DEV, LON_DEV), to_blocks(merged_cot, LAT_DEV // 2, LON_DEV // 2))
    (merge_gain_grad, merge_grad), (merged_blocks, res_blocks, attn_cot_blocks) = lax.scan(merge_block, merge_init, merge_items)
    attn_cot = jnp.roll(from_blocks(attn_cot_blocks), ahead, axis=(0, 1, 2))

    def back_block(carry, item):
        cot_block, block, start = item

        def attend(field, weight_q, weight_p, table):
            return window_attention(field, weight_q, weight_p, table, start, lat_total)
        _, pull = jax.vjp(attend, block, qkv_weight, proj_weight, bias_table)
        field_part, qkv_part, proj_part, table_part = pull(cot_block)
        carry = (carry[0] + qkv_part.astype(jnp.float32), carry[1] + proj_part.astype(jnp.float32), carry[2] + table_part)
        return (carry, field_part)
    back_init = (jnp.zeros(qkv_weight.shape, jnp.float32), jnp.zeros(proj_weight.shape, jnp.float32), jnp.zeros(bias_table.shape, jnp.float32))
    (qkv_grad, proj_grad, bias_grad), field_blocks = lax.scan(back_block, back_init, (to_blocks(attn_cot, LAT_DEV, LON_DEV), shifted_blocks, starts))
    normed_cot = jnp.roll(from_blocks(field_blocks), behind, axis=(0, 1, 2))
    norm_cot, norm_gain_grad = pull_norm(normed_cot)
    features_grad = from_blocks(res_blocks) + norm_cot
    merged = from_blocks(merged_blocks)
    return (merged, features_grad, qkv_grad, proj_grad, merge_grad, norm_gain_grad, merge_gain_grad, bias_grad)
```

```python
import jax
import jax.numpy as jnp
from jax import lax
from jax.sharding import Mesh
from jax.sharding import PartitionSpec as P

HEADS = 8
W_LEV = 2
W_LAT = 6
W_LON = 12


EPSILON = 1e-05
MASKED = -1000000000.0


LON = ("x", "yl", "z")
LAT = ("yh", "c")


def axis_total(axes):
    total = 1
    for axis in axes:
        total *= lax.axis_size(axis)
    return total


def shifted_2(block, axis, distance):
    devices = range(axis_total(axis))
    route = [((i - distance) % len(devices), i) for i in devices]
    return lax.ppermute(block, axis, route)


def normalize(values, gain):
    floats = values.astype(jnp.float32)
    center = floats - jnp.mean(floats, axis=-1, keepdims=True)
    spread = jnp.mean(center * center, axis=-1, keepdims=True)
    return (center * lax.rsqrt(spread + EPSILON) * gain).astype(jnp.bfloat16)


def relative_bias(table):
    window = W_LEV * W_LAT * W_LON
    places = jnp.arange(window, dtype=jnp.int32)
    level_pos = places // (W_LAT * W_LON)
    north_pos = places // W_LON % W_LAT
    east_pos = places % W_LON
    index = (level_pos[:, None] - level_pos[None, :] + W_LEV - 1) * (2 * W_LAT - 1)
    index = (index + north_pos[:, None] - north_pos[None, :] + W_LAT - 1) * (2 * W_LON - 1)
    index = index + east_pos[:, None] - east_pos[None, :] + W_LON - 1
    return jnp.take(table, index, axis=1)


def to_windows(field):
    levels, height, across, width = field.shape
    parted = field.reshape(
        levels // W_LEV, W_LEV, height // W_LAT, W_LAT, across // W_LON, W_LON, width
    )
    return parted.transpose(0, 2, 4, 1, 3, 5, 6).reshape(-1, W_LEV * W_LAT * W_LON, width)


def from_windows(windows, levels, height, across):
    width = windows.shape[-1]
    parted = windows.reshape(
        levels // W_LEV, height // W_LAT, across // W_LON, W_LEV, W_LAT, W_LON, width
    )
    return parted.transpose(0, 3, 1, 4, 2, 5, 6).reshape(levels, height, across, width)


def region_ids(levels, height, across, lat_start, lat_total):
    level_idx = jnp.arange(levels, dtype=jnp.int32)
    level_reg = (level_idx >= levels - W_LEV).astype(jnp.int32) + (
        level_idx >= levels - W_LEV // 2
    ).astype(jnp.int32)
    north_idx = lat_start + jnp.arange(height, dtype=jnp.int32)
    north_reg = (north_idx >= lat_total - W_LAT).astype(jnp.int32) + (
        north_idx >= lat_total - W_LAT // 2
    ).astype(jnp.int32)
    labels = (
        level_reg[:, None, None] * 3
        + north_reg[None, :, None]
        + jnp.zeros((1, 1, across), jnp.int32)
    )
    return to_windows(labels[..., None])[..., 0]


def window_attention(shifted, qkv_weight, proj_weight, table, lat_start, lat_total):
    levels, height, across, width = shifted.shape
    windows = to_windows(shifted)
    count, window = (windows.shape[0], windows.shape[1])
    head_dim = width // HEADS
    packed = jnp.dot(windows.reshape(-1, width), qkv_weight, preferred_element_type=jnp.float32)
    packed = packed.astype(jnp.bfloat16).reshape(count, window, 3, HEADS, head_dim)
    query = packed[:, :, 0]
    key_part = packed[:, :, 1]
    value_part = packed[:, :, 2]
    scores = jnp.einsum(
        "nqhd,nkhd->nhqk", query, key_part, preferred_element_type=jnp.float32
    ) * head_dim ** (-0.5)
    labels = region_ids(levels, height, across, lat_start, lat_total)
    masking = jnp.where(labels[:, :, None] == labels[:, None, :], 0.0, MASKED).astype(jnp.float32)
    scores = scores + relative_bias(table)[None] + masking[:, None]
    weights = jax.nn.softmax(scores, axis=-1).astype(jnp.bfloat16)
    mixed = jnp.einsum("nhqk,nkhd->nqhd", weights, value_part, preferred_element_type=jnp.float32)
    mixed = mixed.astype(jnp.bfloat16).reshape(count * window, width)
    output = jnp.dot(mixed, proj_weight, preferred_element_type=jnp.float32).astype(jnp.bfloat16)
    return from_windows(output.reshape(count, window, width), levels, height, across)


def merge_patches(values, attended, gain, merge_weight):
    summed = (values.astype(jnp.float32) + attended.astype(jnp.float32)).astype(jnp.bfloat16)
    summed = lax.optimization_barrier(summed)
    levels, height, across, width = summed.shape
    stacked = summed.reshape(levels, height // 2, 2, across // 2, 2, width).transpose(
        0, 1, 3, 4, 2, 5
    )
    stacked = stacked.reshape(levels, height // 2, across // 2, 4 * width)
    normed = normalize(stacked, gain)
    return jnp.dot(normed, merge_weight, preferred_element_type=jnp.float32).astype(jnp.bfloat16)


def move_ahead(field):
    east_strip = shifted_2(field[:, :, : W_LON // 2], LON, -1)
    field = jnp.concatenate([field[:, :, W_LON // 2 :], east_strip], axis=2)
    north_strip = shifted_2(field[:, : W_LAT // 2], LAT, -1)
    field = jnp.concatenate([field[:, W_LAT // 2 :], north_strip], axis=1)
    return jnp.roll(field, -(W_LEV // 2), axis=0)


def move_behind(field):
    field = jnp.roll(field, W_LEV // 2, axis=0)
    north_strip = shifted_2(field[:, field.shape[1] - W_LAT // 2 :], LAT, 1)
    field = jnp.concatenate([north_strip, field[:, : field.shape[1] - W_LAT // 2]], axis=1)
    east_strip = shifted_2(field[:, :, field.shape[2] - W_LON // 2 :], LON, 1)
    return jnp.concatenate([east_strip, field[:, :, : field.shape[2] - W_LON // 2]], axis=2)


CORE, NEAR, FAR = ("c",), ("x", "yl"), ("z", "yh")


def exchange(parts, small, axes):
    count = parts.shape[0]
    rows = jnp.broadcast_to(small.astype(jnp.bfloat16)[None], (count,) + small.shape)
    sent = jnp.concatenate([parts.astype(jnp.bfloat16).reshape(count, -1, 128), rows], axis=1)
    got = lax.all_to_all(sent, axes, 0, 0, tiled=True)
    total = jnp.sum(got.astype(jnp.float32), axis=0)
    body = total[: sent.shape[1] - small.shape[0]]
    return body.reshape(parts.shape[1:]), total[sent.shape[1] - small.shape[0] :]


def reduce_all(qkv, proj, merge, vectors):
    def tiles(grad, rows, tiles_wide):
        split = grad.reshape(4, 2, 8, rows, 2, 2, tiles_wide, 128)
        moved = split.transpose(5, 0, 1, 2, 4, 6, 3, 7)
        return moved.reshape(2, 8, 16, tiles_wide * rows, 128)

    parts = jnp.concatenate([tiles(qkv, 8, 3), tiles(proj, 8, 1), tiles(merge, 32, 2)], axis=3)
    small = jnp.concatenate([v.reshape(-1) for v in vectors])
    small = jnp.pad(small, (0, 80 * 128 - small.shape[0])).reshape(80, 128)
    for axes in (CORE, NEAR, FAR):
        parts, small = exchange(parts, small, axes)

    def whole(block, rows, tiles_wide):
        return block.reshape(tiles_wide, rows, 128).transpose(1, 0, 2).reshape(rows, tiles_wide * 128)

    return (
        whole(parts[:24], 8, 3),
        whole(parts[24:32], 8, 1),
        whole(parts[32:], 32, 2),
        small.reshape(-1),
    )


def on_device(
    features, norm_gain, qkv_weight, proj_weight, bias_table, merge_gain, merge_weight, merged_cot
):
    height = features.shape[1]
    lat_total = height * axis_total(LAT)
    lat_start = lax.axis_index(LAT) * height
    normed, pull_norm = jax.vjp(normalize, features, norm_gain)
    shifted = move_ahead(normed)

    def attend(field, weight_q, weight_p, table):
        return window_attention(field, weight_q, weight_p, table, lat_start, lat_total)

    attn_local, pull_attn = jax.vjp(attend, shifted, qkv_weight, proj_weight, bias_table)
    attended = move_behind(attn_local)
    merged, pull_merge = jax.vjp(merge_patches, features, attended, merge_gain, merge_weight)
    res_cot, attn_cot, merge_gain_part, merge_part = pull_merge(merged_cot)
    field_cot, qkv_part, proj_part, table_part = pull_attn(move_ahead(attn_cot))
    norm_cot, norm_gain_part = pull_norm(move_behind(field_cot))
    features_grad = res_cot + norm_cot
    qkv_grad, proj_grad, merge_grad, small = reduce_all(
        qkv_part, proj_part, merge_part, (norm_gain_part, merge_gain_part, table_part)
    )
    norm_gain_grad = small[:512]
    merge_gain_grad = small[512:2560]
    bias_grad = small[2560:8632].reshape(8, 759)
    return (
        merged,
        features_grad,
        qkv_grad,
        proj_grad,
        merge_grad,
        norm_gain_grad,
        merge_gain_grad,
        bias_grad,
    )


def solution(mesh):
    fine = Mesh(mesh.devices.reshape(4, 2, 8, 2, 2), ("x", "yl", "z", "yh", "c"))
    placed = (
        P(None, LAT, LON, None),
        P(),
        P(),
        P(),
        P(),
        P(),
        P(),
        P(None, LAT, LON, None),
    )
    return jax.shard_map(
        on_device,
        mesh=fine,
        in_specs=placed,
        out_specs=(
            P(None, LAT, LON, None),
            P(None, LAT, LON, None),
            P(LON, LAT),
            P(LON, LAT),
            P(LON, LAT),
            P(),
            P(),
            P(),
        ),
        check_vma=False,
    )
```

```python
import functools

import jax
import jax.numpy as jnp
import numpy as np
from jax import lax
from jax.experimental import pallas as pl
from jax.experimental.pallas import tpu as pltpu
from jax.sharding import Mesh
from jax.sharding import PartitionSpec as P

EPSILON = 1e-05
MASKED = -1000000000.0
HEADS, LEV, ROWS, COLS = 8, 4, 6, 12
WIN = 144
TOK = 288
HALF_LON, HALF_LAT = 6, 3
SPAN = 384
TABLE = 759
AXES = ("x", "yl", "z", "yh", "c")
LON, LAT = ("x", "yl", "z"), ("yh", "c")
CORE, NEAR, FAR = ("c",), ("x", "yl"), ("z", "yh")
BF, F32 = jnp.bfloat16, jnp.float32


def token(w, l, r, c):
    return w * WIN + l * 72 + r * 12 + c


def level_of(w, l):
    return (2 * w + l + 1) % LEV


def plans():
    own = np.zeros((TOK, TOK)); west = np.zeros((TOK, 144)); south = np.zeros((TOK, 144))
    back = np.zeros((TOK, TOK))
    quad_own = np.zeros((4 * 96, TOK)); quad_prev = np.zeros((4 * 96, 48)); quad_next = np.zeros((4 * 96, 48))
    edge = np.zeros((96, TOK))
    for w in range(2):
        for l in range(2):
            lev, s = level_of(w, l), 2 * w + l
            for r in range(ROWS):
                for c in range(COLS):
                    t = token(w, l, r, c)
                    i, j = r + HALF_LAT, c + HALF_LON
                    if i >= ROWS:
                        south[t, ((i - ROWS) * COLS + c) * LEV + lev] = 1
                    elif j >= COLS:
                        west[t, (i * HALF_LON + j - COLS) * LEV + lev] = 1
                    else:
                        own[t, (i * COLS + j) * LEV + lev] = 1
                    back[(r * COLS + c) * LEV + lev, t] = 1
                    dj, pc = c % 2, c // 2
                    if r % 2:
                        di, pr = 0, (r + 1) // 2
                    else:
                        di, pr = 1, r // 2
                    quad_own[(dj * 2 + di) * 96 + pr * 24 + s * 6 + pc, t] = 1
                    if r == 0:
                        edge[s * 12 + c, t] = 1
                    if r == ROWS - 1:
                        edge[48 + s * 12 + c, t] = 1
            for c in range(COLS):
                dj, pc = c % 2, c // 2
                quad_prev[(dj * 2 + 0) * 96 + 0 * 24 + s * 6 + pc, s * 12 + c] = 1
                quad_next[(dj * 2 + 1) * 96 + 3 * 24 + s * 6 + pc, s * 12 + c] = 1
    cot_own = np.zeros((96, 72)); cot_west = np.zeros((96, 36)); cot_south = np.zeros((96, 48))
    coarse = np.zeros((72, 96))
    for pr in range(4):
        for s in range(LEV):
            lev = (s + 1) % LEV
            for pc in range(6):
                p = pr * 24 + s * 6 + pc
                i, j = pr + 1, pc + 3
                if i >= 3:
                    cot_south[p, ((i - 3) * 6 + pc) * LEV + lev] = 1
                elif j >= 6:
                    cot_west[p, (i * 3 + j - 6) * LEV + lev] = 1
                else:
                    cot_own[p, (i * 6 + j) * LEV + lev] = 1
                if pr < 3:
                    coarse[(pr * 6 + pc) * LEV + lev, p] = 1
    place = np.zeros(WIN, np.int64)
    for l in range(2):
        for r in range(ROWS):
            for c in range(COLS):
                place[l * 72 + r * 12 + c] = l * 253 + r * 23 + c
    spread = np.zeros((SPAN, 256))
    spread[379 - place, np.arange(WIN)] = 1
    level = np.arange(WIN) // 72
    north = (np.arange(WIN) % 72) // 12 >= HALF_LAT
    return dict(
        own=own, west=west, south=south, back=back, quad_own=quad_own, quad_prev=quad_prev,
        quad_next=quad_next, quad_t=quad_own.T, edge=edge, cot_own=cot_own, cot_west=cot_west,
        cot_south=cot_south, coarse=coarse, spread=spread, spread_t=spread.T,
        apart_level=(level[:, None] != level[None]) * 1.0,
        apart_north=(north[:, None] != north[None]) * 1.0,
    ), [int(v) for v in place]


PLAN, PLACE = plans()


def plan(name):
    return jnp.asarray(PLAN[name], BF)


def mm(a, b):
    return jnp.dot(a, b, preferred_element_type=F32)


def mm_nt(a, b):
    return lax.dot_general(a, b, (((1,), (1,)), ((), ())), preferred_element_type=F32)


def mm_tn(a, b):
    return lax.dot_general(a, b, (((0,), (0,)), ((), ())), preferred_element_type=F32)


def vmem(count):
    return [pl.BlockSpec(memory_space=pltpu.VMEM)] * count


PARAMS = pltpu.CompilerParams(vmem_limit_bytes=56 * 1024 * 1024)


def bias_kernel(last_ref, table_ref, spread_ref, level_ref, north_ref, bias_ref, mask_ref, rows_ref, left_ref, right_ref):
    table = table_ref[...]
    for q in range(WIN):
        rows_ref[8 * q : 8 * q + 8, :] = pltpu.roll(table, (768 - PLACE[q]) % 768, 1)[:, :SPAN]
    rows = rows_ref[...]
    high = rows.astype(BF)
    rest = rows - high.astype(F32)
    middle = rest.astype(BF)
    low = (rest - middle.astype(F32)).astype(BF)
    spread = spread_ref[...]
    wide = mm(high, spread) + mm(middle, spread) + mm(low, spread)
    left_ref[...] = wide[:, :128]
    right_ref[...] = wide[:, 128:]
    for h in range(HEADS):
        bias_ref[h, :, :128] = left_ref[pl.ds(h, WIN, stride=8), :]
        bias_ref[h, :, 128:] = right_ref[pl.ds(h, WIN, stride=8), :][:, :16]
    north = jnp.where(last_ref[0] == 1, north_ref[...].astype(F32), 0.0)
    mask_ref[0] = north * MASKED
    mask_ref[1] = jnp.maximum(north, level_ref[...].astype(F32)) * MASKED


def bias_of(table, last):
    shapes = [jax.ShapeDtypeStruct((HEADS, WIN, WIN), F32), jax.ShapeDtypeStruct((2, WIN, WIN), F32)]
    return pl.pallas_call(
        bias_kernel,
        out_shape=shapes,
        in_specs=[pl.BlockSpec(memory_space=pltpu.SMEM)] + vmem(4),
        out_specs=vmem(2),
        scratch_shapes=[pltpu.VMEM((8 * WIN, SPAN), F32)] + [pltpu.VMEM((8 * WIN, 128), F32)] * 2,
        compiler_params=PARAMS,
    )(last, jnp.pad(table, ((0, 0), (0, 768 - TABLE))), plan("spread"), plan("apart_level"), plan("apart_north"))


def norm_parts(values, width):
    mean = sum(jnp.sum(v, axis=1, keepdims=True) for v in values) * (1.0 / width)
    center = [v - mean for v in values]
    spread = sum(jnp.sum(v * v, axis=1, keepdims=True) for v in center) * (1.0 / width)
    scale = lax.rsqrt(spread + EPSILON)
    return [v * scale for v in center], scale


def norm_back(hats, scale, cots, gains, width):
    inner = [c * g for c, g in zip(cots, gains)]
    first = sum(jnp.sum(v, axis=1, keepdims=True) for v in inner) * (1.0 / width)
    second = sum(jnp.sum(v * h, axis=1, keepdims=True) for v, h in zip(inner, hats)) * (1.0 / width)
    return [scale * (v - first - h * second) for v, h in zip(inner, hats)]


def lower_half():
    return lax.broadcasted_iota(jnp.int32, (WIN, 128), 1) < 64


def attend_kernel(
    own_ref, west_ref, south_ref, plan_own, plan_west, plan_south, plan_edge, gain_ref, wqkv_ref, wproj_ref,
    bias_ref, mask_ref, x_ref, qkv_ref, p_ref, mixed_ref, block_ref, edge_ref,
):
    x = mm(plan_own[...], own_ref[...]) + mm(plan_west[...], west_ref[...]) + mm(plan_south[...], south_ref[...])
    x_ref[...] = x.astype(BF)
    (hat,), _ = norm_parts([x], 512)
    normed = (hat * gain_ref[...]).astype(BF)
    qkv_ref[...] = mm(normed, wqkv_ref[...]).astype(BF)
    lower = lower_half()
    for w in range(2):
        rows = slice(w * WIN, (w + 1) * WIN)
        for pair in range(4):
            lanes = slice(pair * 128, pair * 128 + 128)
            query = qkv_ref[rows, lanes]
            key = qkv_ref[rows, 512 + pair * 128 : 640 + pair * 128]
            value = qkv_ref[rows, 1024 + pair * 128 : 1152 + pair * 128]
            outs = []
            for half in range(2):
                h = 2 * pair + half
                keep = lower if half == 0 else jnp.logical_not(lower)
                part = jnp.where(keep, query * 0.125, 0.0).astype(BF)
                scores = mm_nt(part, key) + bias_ref[h] + mask_ref[w]
                top = jnp.max(scores, axis=1, keepdims=True)
                grown = jnp.exp(scores - top)
                weights = (grown / jnp.sum(grown, axis=1, keepdims=True)).astype(BF)
                p_ref[w * HEADS + h] = weights
                outs.append(mm(weights, value))
            mixed_ref[rows, lanes] = jnp.where(lower, outs[0], outs[1]).astype(BF)
    attended = mm(mixed_ref[...], wproj_ref[...]).astype(BF)
    block = (x + attended.astype(F32)).astype(BF)
    block_ref[...] = block
    edge_ref[...] = mm(plan_edge[...], block).astype(BF)


def attend(own, west, south, gain, wqkv, wproj, bias, mask):
    shapes = [(TOK, 512), (TOK, 1536), (2 * HEADS, WIN, WIN), (TOK, 512), (TOK, 512), (96, 512)]
    return pl.pallas_call(
        attend_kernel,
        out_shape=[jax.ShapeDtypeStruct(s, BF) for s in shapes],
        in_specs=vmem(12),
        out_specs=vmem(6),
        compiler_params=PARAMS,
    )(own, west, south, plan("own"), plan("west"), plan("south"), plan("edge"), gain, wqkv, wproj, bias, mask)


def merge_kernel(
    block_ref, prev_ref, next_ref, cot_ref, cot_west_ref, cot_south_ref, quad_own, quad_prev, quad_next, quad_t,
    plan_cot, plan_cot_west, plan_cot_south, coarse, gain_ref, wmerge_ref,
    merged_ref, back_ref, gain_grad_ref, parts_ref,
):
    stacked = mm(quad_own[...], block_ref[...]) + mm(quad_prev[...], prev_ref[...]) + mm(quad_next[...], next_ref[...])
    values = [stacked[96 * k : 96 * k + 96] for k in range(4)]
    hats, scale = norm_parts(values, 2048)
    gains = [gain_ref[:, 512 * k : 512 * k + 512] for k in range(4)]
    normed = [(h * g).astype(BF) for h, g in zip(hats, gains)]
    merged = sum(mm(normed[k], wmerge_ref[512 * k : 512 * k + 512, :]) for k in range(4)).astype(BF)
    merged_ref[...] = mm(coarse[...], merged).astype(BF)
    cot = (
        mm(plan_cot[...], cot_ref[...]) + mm(plan_cot_west[...], cot_west_ref[...])
        + mm(plan_cot_south[...], cot_south_ref[...])
    )
    cot_all = cot.astype(BF)
    counted = lax.broadcasted_iota(jnp.int32, (96, 1024), 0) < 72
    cot_own = jnp.where(counted, cot, 0.0).astype(BF)
    cots = [mm_nt(cot_all, wmerge_ref[512 * k : 512 * k + 512, :]).astype(BF).astype(F32) for k in range(4)]
    for k in range(4):
        gain_grad_ref[:, 512 * k : 512 * k + 512] = jnp.sum((cots[k] * hats[k])[:72], axis=0, keepdims=True)
    pulled = norm_back(hats, scale, cots, gains, 2048)
    back_ref[...] = mm(quad_t[...], jnp.concatenate(pulled, axis=0).astype(BF)).astype(BF)
    for k in range(4):
        for lat in range(4):
            grad = mm_tn(normed[k], cot_own[:, 256 * lat : 256 * lat + 256])
            for t in range(2):
                piece = grad[:, 128 * t : 128 * t + 128].reshape(2, 8, 32, 128).astype(BF)
                parts_ref[lat % 2, 2 * k : 2 * k + 2, :, lat // 2, 32 * t : 32 * t + 32, :] = piece


def merge(block, prev, following, cot, cot_west, cot_south, gain, wmerge):
    shapes = [
        jax.ShapeDtypeStruct((72, 1024), BF), jax.ShapeDtypeStruct((TOK, 512), BF),
        jax.ShapeDtypeStruct((1, 2048), F32), jax.ShapeDtypeStruct((2, 8, 8, 2, 64, 128), BF),
    ]
    names = ("quad_own", "quad_prev", "quad_next", "quad_t", "cot_own", "cot_west", "cot_south", "coarse")
    return pl.pallas_call(
        merge_kernel,
        out_shape=shapes,
        in_specs=vmem(16),
        out_specs=vmem(4),
        compiler_params=PARAMS,
    )(block, prev, following, cot, cot_west, cot_south, *[plan(n) for n in names], gain, wmerge)


def back_kernel(
    cot_ref, x_ref, qkv_ref, p_ref, mixed_ref, wqkv_ref, wproj_ref, gain_ref, spread_t, back_plan,
    grad_ref, gain_grad_ref, bias_grad_ref, parts_ref, dqkv_ref, left_ref, right_ref, wide_ref,
):
    cot = cot_ref[...]
    mixed_cot = mm_nt(cot, wproj_ref[...]).astype(BF)
    lower = lower_half()
    for w in range(2):
        rows = slice(w * WIN, (w + 1) * WIN)
        for pair in range(4):
            lanes = slice(pair * 128, pair * 128 + 128)
            query = qkv_ref[rows, lanes]
            key = qkv_ref[rows, 512 + pair * 128 : 640 + pair * 128]
            value = qkv_ref[rows, 1024 + pair * 128 : 1152 + pair * 128]
            out_cot = mixed_cot[rows, lanes]
            found = []
            for half in range(2):
                h = 2 * pair + half
                keep = lower if half == 0 else jnp.logical_not(lower)
                part = jnp.where(keep, out_cot, 0.0).astype(BF)
                weights = p_ref[w * HEADS + h]
                weight_cot = mm_nt(part, value).astype(BF).astype(F32)
                wide = weights.astype(F32)
                product = wide * weight_cot
                score_cot = product - wide * jnp.sum(product, axis=1, keepdims=True)
                places = pl.ds(h, WIN, stride=8)
                right = jnp.concatenate([score_cot[:, 128:], jnp.zeros((WIN, 112), F32)], axis=1)
                if w == 0:
                    left_ref[places, :] = score_cot[:, :128]
                    right_ref[places, :] = right
                else:
                    left_ref[places, :] = left_ref[places, :] + score_cot[:, :128]
                    right_ref[places, :] = right_ref[places, :] + right
                scaled = (score_cot * 0.125).astype(BF)
                found.append((mm(scaled, key), mm_tn(scaled, query), mm_tn(weights, out_cot)))
            for n in range(3):
                both = jnp.where(lower, found[0][n], found[1][n]).astype(BF)
                dqkv_ref[rows, 512 * n + pair * 128 : 512 * n + pair * 128 + 128] = both
    dqkv = dqkv_ref[...]
    x = x_ref[...].astype(F32)
    (hat,), scale = norm_parts([x], 512)
    gain = gain_ref[...]
    normed = (hat * gain).astype(BF)
    normed_cot = mm_nt(dqkv, wqkv_ref[...]).astype(BF).astype(F32)
    gain_grad_ref[...] = jnp.sum(normed_cot * hat, axis=0, keepdims=True)
    (pulled,) = norm_back([hat], scale, [normed_cot], [gain], 512)
    total = (cot.astype(F32) + pulled.astype(BF).astype(F32)).astype(BF)
    grad_ref[...] = mm(back_plan[...], total).astype(BF)
    mixed = mixed_ref[...]
    for lat in range(4):
        grad = mm_tn(normed, dqkv[:, 384 * lat : 384 * lat + 384])
        proj = mm_tn(mixed, cot[:, 128 * lat : 128 * lat + 128])
        tiles = [grad[:, 128 * t : 128 * t + 128].reshape(8, 8, 8, 128) for t in range(3)] + [proj.reshape(8, 8, 8, 128)]
        for t in range(2):
            piece = jnp.concatenate([tiles[2 * t], tiles[2 * t + 1]], axis=2).astype(BF)
            parts_ref[lat % 2, :, :, lat // 2, 16 * t : 16 * t + 16, :] = piece
    wide_ref[...] = mm(left_ref[...].astype(BF), spread_t[:128, :]) + mm(right_ref[...].astype(BF), spread_t[128:, :])
    blank = jnp.zeros((8, 512 - SPAN), F32)
    levels = []
    for l in range(2):
        outer = None
        for r in reversed(range(ROWS)):
            inner = None
            for c in reversed(range(COLS)):
                q = 8 * (l * 72 + r * 12 + c)
                here = jnp.concatenate([wide_ref[q : q + 8, :], blank], axis=1)
                inner = here if inner is None else pltpu.roll(inner, 1, 1) + here
            outer = inner if outer is None else pltpu.roll(outer, 23, 1) + inner
        levels.append(jnp.concatenate([outer, jnp.zeros((8, 256), F32)], axis=1))
    bias_grad_ref[...] = levels[0] + pltpu.roll(levels[1], 253, 1)


def attend_back(cot, x, qkv, p, mixed, wqkv, wproj, gain):
    shapes = [
        jax.ShapeDtypeStruct((TOK, 512), BF), jax.ShapeDtypeStruct((1, 512), F32),
        jax.ShapeDtypeStruct((8, 768), F32), jax.ShapeDtypeStruct((2, 8, 8, 2, 32, 128), BF),
    ]
    return pl.pallas_call(
        back_kernel,
        out_shape=shapes,
        in_specs=vmem(10),
        out_specs=vmem(4),
        scratch_shapes=[pltpu.VMEM((TOK, 1536), BF), pltpu.VMEM((8 * WIN, 128), F32), pltpu.VMEM((8 * WIN, 128), F32), pltpu.VMEM((8 * WIN, SPAN), F32)],
        compiler_params=PARAMS,
    )(cot, x, qkv, p, mixed, wqkv, wproj, gain, plan("spread_t"), plan("back"))


def total_of(axes):
    total = 1
    for axis in axes:
        total *= lax.axis_size(axis)
    return total


def moved(block, axes, distance):
    count = total_of(axes)
    return lax.ppermute(block, axes, [((i - distance) % count, i) for i in range(count)])


def exchange(parts, small, axes):
    count = parts.shape[0]
    rows = jnp.broadcast_to(small.astype(BF)[None], (count,) + small.shape)
    sent = jnp.concatenate([parts.astype(BF).reshape(count, -1, 128), rows], axis=1)
    got = lax.all_to_all(sent, axes, 0, 0, tiled=True)
    total = jnp.sum(got.astype(F32), axis=0)
    body = total[: sent.shape[1] - small.shape[0]]
    return body.reshape(parts.shape[1:]), total[sent.shape[1] - small.shape[0] :]


def reduce_all(early, late, vectors):
    parts = jnp.concatenate([late, early], axis=4).reshape(2, 8, 16, 96, 128)
    small = jnp.concatenate([v.reshape(-1, 128) for v in vectors], axis=0)
    small = jnp.pad(small, ((0, 80 - small.shape[0]), (0, 0)))
    for axes in (CORE, NEAR, FAR):
        parts, small = exchange(parts, small, axes)

    def whole(block, rows, tiles_wide):
        return block.reshape(tiles_wide, rows, 128).transpose(1, 0, 2).reshape(rows, tiles_wide * 128)

    return whole(parts[:24], 8, 3), parts[24:32], whole(parts[32:], 32, 2), small


def on_device(features, norm_gain, qkv_weight, proj_weight, bias_table, merge_gain, merge_weight, merged_cot):
    last = (lax.axis_index(LAT) == total_of(LAT) - 1).astype(jnp.int32).reshape(1)
    gain, wide_gain = norm_gain.reshape(1, 512), merge_gain.reshape(1, 2048)
    own = features.transpose(1, 2, 0, 3).reshape(6, 48, 512)
    cot = merged_cot.transpose(1, 2, 0, 3).reshape(3, 24, 1024)
    west = moved(own[:, :24], LON, -1)
    cot_west = moved(cot[:, :12], LON, -1)
    south = moved(jnp.concatenate([own[:3, 24:], west[:3]], axis=1), LAT, -1)
    cot_south = moved(jnp.concatenate([cot[:2, 12:], cot_west[:2]], axis=1), LAT, -1)
    bias, mask = bias_of(bias_table, last)
    x, qkv, p, mixed, block, edge = attend(
        own.reshape(TOK, 512), west.reshape(144, 512), south.reshape(144, 512), gain, qkv_weight, proj_weight, bias, mask
    )
    following = moved(edge[:48], LAT, -1)
    prev = moved(edge[48:], LAT, 1)
    merged, attn_cot, merge_gain_part, early = merge(
        block, prev, following, cot.reshape(72, 1024), cot_west.reshape(36, 1024), cot_south.reshape(48, 1024),
        wide_gain, merge_weight,
    )
    grad, norm_gain_part, bias_part, late = attend_back(
        attn_cot, x, qkv, p, mixed, qkv_weight, proj_weight, gain
    )

    def home(field, rows_back, width_back):
        north = moved(field[field.shape[0] - rows_back :], LAT, 1)
        field = jnp.concatenate([north, field[: field.shape[0] - rows_back]], axis=0)
        east = moved(field[:, field.shape[1] - width_back :], LON, 1)
        return jnp.concatenate([east, field[:, : field.shape[1] - width_back]], axis=1)

    merged = home(merged.reshape(3, 24, 1024), 1, 12).reshape(3, 6, 4, 1024).transpose(2, 0, 1, 3)
    features_grad = home(grad.reshape(6, 48, 512), 3, 24).reshape(6, 12, 4, 512).transpose(2, 0, 1, 3)
    qkv_grad, proj_grad, merge_grad, small = reduce_all(early, late, (norm_gain_part, merge_gain_part, bias_part))
    return (
        merged,
        features_grad,
        qkv_grad,
        proj_grad,
        merge_grad,
        small[:4].reshape(-1),
        small[4:20].reshape(-1),
        small[20:68].reshape(8, 768)[:, :TABLE],
    )


def solution(mesh):
    fine = Mesh(mesh.devices.reshape(4, 2, 8, 2, 2), AXES)
    field = P(None, LAT, LON, None)
    return jax.shard_map(
        on_device,
        mesh=fine,
        in_specs=(field, P(), P(), P(), P(), P(), P(), field),
        out_specs=(field, field, P(LON, LAT), P(LON, LAT), P(LON, LAT), P(), P(), P()),
        check_vma=False,
    )
```

```python
import functools

import jax
import jax.numpy as jnp
import numpy as np
from jax import lax
from jax.experimental import pallas as pl
from jax.experimental.pallas import tpu as pltpu
from jax.sharding import Mesh
from jax.sharding import PartitionSpec as P

EPSILON = 1e-05
MASKED = -1000000000.0
HEADS, LEV, ROWS, COLS = 8, 4, 6, 12
WIN = 144
TOK = 288
HALF_LON, HALF_LAT = 6, 3
SPAN = 384
TABLE = 759
AXES = ("x", "yl", "z", "yh", "c")
LON, LAT = ("x", "yl", "z"), ("yh", "c")
NEAR, FAR, CLOSE = ("x", "yl"), ("z", "yh"), ("x", "yl", "c")
BF, F32 = jnp.bfloat16, jnp.float32


def token(w, l, r, c):
    return w * WIN + l * 72 + r * 12 + c


def level_of(w, l):
    return (2 * w + l + 1) % LEV


def plans():
    own = np.zeros((TOK, TOK)); west = np.zeros((TOK, 144)); south = np.zeros((TOK, 72)); corner = np.zeros((TOK, 72))
    back = np.zeros((TOK, TOK))
    quad_own = np.zeros((4 * 96, TOK)); quad_prev = np.zeros((4 * 96, 48)); quad_next = np.zeros((4 * 96, 48))
    edge = np.zeros((96, TOK))
    for w in range(2):
        for l in range(2):
            lev, s = level_of(w, l), 2 * w + l
            for r in range(ROWS):
                for c in range(COLS):
                    t = token(w, l, r, c)
                    i, j = r + HALF_LAT, c + HALF_LON
                    if i >= ROWS and j >= COLS:
                        corner[t, ((i - ROWS) * HALF_LON + j - COLS) * LEV + lev] = 1
                    elif i >= ROWS:
                        south[t, ((i - ROWS) * HALF_LON + c) * LEV + lev] = 1
                    elif j >= COLS:
                        west[t, (i * HALF_LON + j - COLS) * LEV + lev] = 1
                    else:
                        own[t, (i * COLS + j) * LEV + lev] = 1
                    back[(r * COLS + c) * LEV + lev, t] = 1
                    dj, pc = c % 2, c // 2
                    if r % 2:
                        di, pr = 0, (r + 1) // 2
                    else:
                        di, pr = 1, r // 2
                    quad_own[(dj * 2 + di) * 96 + pr * 24 + s * 6 + pc, t] = 1
                    if r == 0:
                        edge[s * 12 + c, t] = 1
                    if r == ROWS - 1:
                        edge[48 + s * 12 + c, t] = 1
            for c in range(COLS):
                dj, pc = c % 2, c // 2
                quad_prev[(dj * 2 + 0) * 96 + 0 * 24 + s * 6 + pc, s * 12 + c] = 1
                quad_next[(dj * 2 + 1) * 96 + 3 * 24 + s * 6 + pc, s * 12 + c] = 1
    cot_own = np.zeros((96, 72)); cot_west = np.zeros((96, 24)); cot_south = np.zeros((96, 24)); cot_corner = np.zeros((96, 24))
    coarse = np.zeros((72, 96))
    for pr in range(4):
        for s in range(LEV):
            lev = (s + 1) % LEV
            for pc in range(6):
                p = pr * 24 + s * 6 + pc
                i, j = pr + 1, pc + 3
                if i >= 3 and j >= 6:
                    cot_corner[p, ((i - 3) * 3 + j - 6) * LEV + lev] = 1
                elif i >= 3:
                    cot_south[p, ((i - 3) * 3 + pc) * LEV + lev] = 1
                elif j >= 6:
                    cot_west[p, ((i - 1) * 3 + j - 6) * LEV + lev] = 1
                else:
                    cot_own[p, (i * 6 + j) * LEV + lev] = 1
                if pr < 3:
                    coarse[(pr * 6 + pc) * LEV + lev, p] = 1
    place = np.zeros(WIN, np.int64)
    for l in range(2):
        for r in range(ROWS):
            for c in range(COLS):
                place[l * 72 + r * 12 + c] = l * 253 + r * 23 + c
    spread = np.zeros((SPAN, 256))
    spread[379 - place, np.arange(WIN)] = 1
    level = np.arange(WIN) // 72
    north = (np.arange(WIN) % 72) // 12 >= HALF_LAT
    return dict(
        own=own, west=west, south=south, corner=corner, back=back, quad_own=quad_own, quad_prev=quad_prev,
        quad_next=quad_next, quad_t=quad_own.T, edge=edge, cot_own=cot_own, cot_west=cot_west,
        cot_south=cot_south, cot_corner=cot_corner, coarse=coarse, spread=spread, spread_t=spread.T,
        apart_level=(level[:, None] != level[None]) * 1.0,
        apart_north=(north[:, None] != north[None]) * 1.0,
    ), [int(v) for v in place]


PLAN, PLACE = plans()


def plan(name):
    return jnp.asarray(PLAN[name], BF)


def mm(a, b):
    return jnp.dot(a, b, preferred_element_type=F32)


def mm_nt(a, b):
    return lax.dot_general(a, b, (((1,), (1,)), ((), ())), preferred_element_type=F32)


def mm_tn(a, b):
    return lax.dot_general(a, b, (((0,), (0,)), ((), ())), preferred_element_type=F32)


def vmem(count):
    return [pl.BlockSpec(memory_space=pltpu.VMEM)] * count


def cost(flops, moved_bytes):
    return pl.CostEstimate(flops=flops, bytes_accessed=moved_bytes, transcendentals=0)


PARAMS = pltpu.CompilerParams(vmem_limit_bytes=56 * 1024 * 1024)


def bias_kernel(last_ref, table_ref, spread_ref, level_ref, north_ref, bias_ref, mask_ref, rows_ref, left_ref, right_ref):
    table = table_ref[...]
    for q in range(WIN):
        rows_ref[8 * q : 8 * q + 8, :] = pltpu.roll(table, (768 - PLACE[q]) % 768, 1)[:, :SPAN]
    rows = rows_ref[...]
    high = rows.astype(BF)
    rest = rows - high.astype(F32)
    middle = rest.astype(BF)
    low = (rest - middle.astype(F32)).astype(BF)
    spread = spread_ref[...]
    wide = mm(high, spread) + mm(middle, spread) + mm(low, spread)
    left_ref[...] = wide[:, :128]
    right_ref[...] = wide[:, 128:]
    for h in range(HEADS):
        bias_ref[h, :, :128] = left_ref[pl.ds(h, WIN, stride=8), :]
        bias_ref[h, :, 128:] = right_ref[pl.ds(h, WIN, stride=8), :][:, :16]
    north = jnp.where(last_ref[0] == 1, north_ref[...].astype(F32), 0.0)
    mask_ref[0] = north * MASKED
    mask_ref[1] = jnp.maximum(north, level_ref[...].astype(F32)) * MASKED


def bias_of(table, last):
    shapes = [jax.ShapeDtypeStruct((HEADS, WIN, WIN), F32), jax.ShapeDtypeStruct((2, WIN, WIN), F32)]
    return pl.pallas_call(
        bias_kernel,
        out_shape=shapes,
        in_specs=[pl.BlockSpec(memory_space=pltpu.SMEM)] + vmem(4),
        out_specs=vmem(2),
        scratch_shapes=[pltpu.VMEM((8 * WIN, SPAN), F32)] + [pltpu.VMEM((8 * WIN, 128), F32)] * 2,
        compiler_params=PARAMS,
        cost_estimate=cost(2_000_000_000, 4_000_000),
    )(last, jnp.pad(table, ((0, 0), (0, 768 - TABLE))), plan("spread"), plan("apart_level"), plan("apart_north"))


def norm_parts(values, width):
    mean = sum(jnp.sum(v, axis=1, keepdims=True) for v in values) * (1.0 / width)
    center = [v - mean for v in values]
    spread = sum(jnp.sum(v * v, axis=1, keepdims=True) for v in center) * (1.0 / width)
    scale = lax.rsqrt(spread + EPSILON)
    return [v * scale for v in center], scale


def norm_back(hats, scale, cots, gains, width):
    inner = [c * g for c, g in zip(cots, gains)]
    first = sum(jnp.sum(v, axis=1, keepdims=True) for v in inner) * (1.0 / width)
    second = sum(jnp.sum(v * h, axis=1, keepdims=True) for v, h in zip(inner, hats)) * (1.0 / width)
    return [scale * (v - first - h * second) for v, h in zip(inner, hats)]


def lower_half():
    return lax.broadcasted_iota(jnp.int32, (WIN, 128), 1) < 64


def attend_kernel(
    own_ref, west_ref, south_ref, corner_ref, plan_own, plan_west, plan_south, plan_corner, plan_edge, gain_ref, wqkv_ref, wproj_ref,
    bias_ref, mask_ref, x_ref, qkv_ref, p_ref, mixed_ref, block_ref, first_ref, last_ref,
):
    x = (
        mm(plan_own[...], own_ref[...]) + mm(plan_west[...], west_ref[...])
        + mm(plan_south[...], south_ref[...]) + mm(plan_corner[...], corner_ref[...])
    )
    x_ref[...] = x.astype(BF)
    (hat,), _ = norm_parts([x], 512)
    normed = (hat * gain_ref[...]).astype(BF)
    qkv_ref[...] = mm(normed, wqkv_ref[...]).astype(BF)
    lower = lower_half()
    for w in range(2):
        rows = slice(w * WIN, (w + 1) * WIN)
        for pair in range(4):
            lanes = slice(pair * 128, pair * 128 + 128)
            query = qkv_ref[rows, lanes]
            key = qkv_ref[rows, 512 + pair * 128 : 640 + pair * 128]
            value = qkv_ref[rows, 1024 + pair * 128 : 1152 + pair * 128]
            outs = []
            for half in range(2):
                h = 2 * pair + half
                keep = lower if half == 0 else jnp.logical_not(lower)
                part = jnp.where(keep, query * 0.125, 0.0).astype(BF)
                scores = mm_nt(part, key) + bias_ref[h] + mask_ref[w]
                top = jnp.max(scores, axis=1, keepdims=True)
                grown = jnp.exp(scores - top)
                weights = (grown / jnp.sum(grown, axis=1, keepdims=True)).astype(BF)
                p_ref[w * HEADS + h] = weights
                outs.append(mm(weights, value))
            mixed_ref[rows, lanes] = jnp.where(lower, outs[0], outs[1]).astype(BF)
    attended = mm(mixed_ref[...], wproj_ref[...]).astype(BF)
    block = (x + attended.astype(F32)).astype(BF)
    block_ref[...] = block
    edge = mm(plan_edge[...], block).astype(BF)
    first_ref[...] = edge[:48]
    last_ref[...] = edge[48:]


def attend(own, west, south, corner, gain, wqkv, wproj, bias, mask):
    shapes = [(TOK, 512), (TOK, 1536), (2 * HEADS, WIN, WIN), (TOK, 512), (TOK, 512), (48, 512), (48, 512)]
    return pl.pallas_call(
        attend_kernel,
        out_shape=[jax.ShapeDtypeStruct(s, BF) for s in shapes],
        in_specs=vmem(14),
        out_specs=vmem(7),
        compiler_params=PARAMS,
        cost_estimate=cost(4_000_000_000, 8_000_000),
    )(own, west, south, corner, plan("own"), plan("west"), plan("south"), plan("corner"), plan("edge"), gain, wqkv, wproj, bias, mask)


def stack_kernel(
    block_ref, prev_ref, next_ref, cot_ref, cot_west_ref, cot_south_ref, cot_corner_ref, quad_own, quad_prev, quad_next,
    plan_cot, plan_cot_west, plan_cot_south, plan_cot_corner, gain_ref, pair_ref, hats_ref, scale_ref, all_cot_ref,
):
    stacked = mm(quad_own[...], block_ref[...]) + mm(quad_prev[...], prev_ref[...]) + mm(quad_next[...], next_ref[...])
    values = [stacked[96 * k : 96 * k + 96] for k in range(4)]
    hats, scale = norm_parts(values, 2048)
    scale_ref[...] = jnp.broadcast_to(scale, (96, 128))
    normed = []
    for k in range(4):
        hats_ref[k] = hats[k]
        normed.append((hats[k] * gain_ref[:, 512 * k : 512 * k + 512]).astype(BF))
    cot = (
        mm(plan_cot[...], cot_ref[...]) + mm(plan_cot_west[...], cot_west_ref[...])
        + mm(plan_cot_south[...], cot_south_ref[...]) + mm(plan_cot_corner[...], cot_corner_ref[...])
    )
    all_cot_ref[...] = cot.astype(BF)
    counted = lax.broadcasted_iota(jnp.int32, (80, 1024), 0) < 72
    cot_own = jnp.where(counted, cot[:80], 0.0).astype(BF)
    for c in range(2):
        halves = [cot_own[:, 512 * yh + 256 * c : 512 * yh + 256 * c + 256] for yh in range(2)]
        for xy in range(8):
            peer = 2 * xy + c
            pair_ref[peer, :, :256] = normed[xy // 2][:80, 256 * (xy % 2) : 256 * (xy % 2) + 256]
            pair_ref[peer, :, 256:512] = halves[0]
            pair_ref[peer, :, 512:] = halves[1]


def stack(block, prev, following, cot, cot_west, cot_south, cot_corner, gain):
    shapes = [
        jax.ShapeDtypeStruct((16, 80, 768), BF), jax.ShapeDtypeStruct((4, 96, 512), F32),
        jax.ShapeDtypeStruct((96, 128), F32), jax.ShapeDtypeStruct((96, 1024), BF),
    ]
    names = ("quad_own", "quad_prev", "quad_next", "cot_own", "cot_west", "cot_south", "cot_corner")
    return pl.pallas_call(
        stack_kernel,
        out_shape=shapes,
        in_specs=vmem(15),
        out_specs=vmem(4),
        compiler_params=PARAMS,
        cost_estimate=cost(2_000_000_000, 8_000_000),
    )(block, prev, following, cot, cot_west, cot_south, cot_corner, *[plan(n) for n in names], gain)


def merge_kernel(
    hats_ref, scale_ref, all_cot_ref, quad_t, coarse, gain_ref, wmerge_ref, merged_ref, back_ref, gain_grad_ref,
):
    gains = [gain_ref[:, 512 * k : 512 * k + 512] for k in range(4)]
    hats = [hats_ref[k] for k in range(4)]
    scale = scale_ref[:, :1]
    cot_all = all_cot_ref[...]
    cots = [mm_nt(cot_all, wmerge_ref[512 * k : 512 * k + 512, :]).astype(BF).astype(F32) for k in range(4)]
    pulled = norm_back(hats, scale, cots, gains, 2048)
    back_ref[...] = mm(quad_t[...], jnp.concatenate(pulled, axis=0).astype(BF)).astype(BF)
    normed = [(h * g).astype(BF) for h, g in zip(hats, gains)]
    merged = sum(mm(normed[k], wmerge_ref[512 * k : 512 * k + 512, :]) for k in range(4)).astype(BF)
    merged_ref[...] = mm(coarse[...], merged).astype(BF)
    for k in range(4):
        summed = jnp.sum((cots[k] * hats[k])[:72], axis=0, keepdims=True)
        for i in range(4):
            gain_grad_ref[4 * k + i : 4 * k + i + 1, :] = summed[:, 128 * i : 128 * i + 128]


def merge(hats, scale, all_cot, gain, wmerge):
    shapes = [
        jax.ShapeDtypeStruct((72, 1024), BF), jax.ShapeDtypeStruct((TOK, 512), BF),
        jax.ShapeDtypeStruct((16, 128), F32),
    ]
    return pl.pallas_call(
        merge_kernel,
        out_shape=shapes,
        in_specs=vmem(7),
        out_specs=vmem(3),
        compiler_params=PARAMS,
        cost_estimate=cost(4_000_000_000, 16_000_000),
    )(hats, scale, all_cot, plan("quad_t"), plan("coarse"), gain, wmerge)


def back_kernel(
    core_ref, cot_ref, x_ref, qkv_ref, p_ref, mixed_ref, wqkv_ref, wproj_ref, gain_ref, merge_gain_ref, spread_t, back_plan,
    grad_ref, small_ref, mine_ref, theirs_ref, dqkv_ref, left_ref, right_ref, wide_ref,
):
    cot = cot_ref[...]
    mixed_cot = mm_nt(cot, wproj_ref[...]).astype(BF)
    lower = lower_half()
    for w in range(2):
        rows = slice(w * WIN, (w + 1) * WIN)
        for pair in range(4):
            lanes = slice(pair * 128, pair * 128 + 128)
            query = qkv_ref[rows, lanes]
            key = qkv_ref[rows, 512 + pair * 128 : 640 + pair * 128]
            value = qkv_ref[rows, 1024 + pair * 128 : 1152 + pair * 128]
            out_cot = mixed_cot[rows, lanes]
            found = []
            for half in range(2):
                h = 2 * pair + half
                keep = lower if half == 0 else jnp.logical_not(lower)
                part = jnp.where(keep, out_cot, 0.0).astype(BF)
                weights = p_ref[w * HEADS + h]
                weight_cot = mm_nt(part, value).astype(BF).astype(F32)
                wide = weights.astype(F32)
                product = wide * weight_cot
                score_cot = product - wide * jnp.sum(product, axis=1, keepdims=True)
                places = pl.ds(h, WIN, stride=8)
                right = jnp.concatenate([score_cot[:, 128:], jnp.zeros((WIN, 112), F32)], axis=1)
                if w == 0:
                    left_ref[places, :] = score_cot[:, :128]
                    right_ref[places, :] = right
                else:
                    left_ref[places, :] = left_ref[places, :] + score_cot[:, :128]
                    right_ref[places, :] = right_ref[places, :] + right
                scaled = (score_cot * 0.125).astype(BF)
                found.append((mm(scaled, key), mm_tn(scaled, query), mm_tn(weights, out_cot)))
            for n in range(3):
                both = jnp.where(lower, found[0][n], found[1][n]).astype(BF)
                dqkv_ref[rows, 512 * n + pair * 128 : 512 * n + pair * 128 + 128] = both
    dqkv = dqkv_ref[...]
    x = x_ref[...].astype(F32)
    (hat,), scale = norm_parts([x], 512)
    gain = gain_ref[...]
    normed = (hat * gain).astype(BF)
    normed_cot = mm_nt(dqkv, wqkv_ref[...]).astype(BF).astype(F32)
    gain_grad = jnp.sum(normed_cot * hat, axis=0, keepdims=True)
    small_ref[48:64, :] = merge_gain_ref[...]
    small_ref[64:80, :] = jnp.zeros((16, 128), F32)
    for i in range(4):
        small_ref[64 + i : 65 + i, :] = gain_grad[:, 128 * i : 128 * i + 128]
    (pulled,) = norm_back([hat], scale, [normed_cot], [gain], 512)
    total = (cot.astype(F32) + pulled.astype(BF).astype(F32)).astype(BF)
    grad_ref[...] = mm(back_plan[...], total).astype(BF)
    mixed = mixed_ref[...]
    core = core_ref[0]
    for yh in range(2):
        for out_ref, owner in ((theirs_ref, 1 - core), (mine_ref, core)):
            first = pl.multiple_of(768 * yh + 384 * owner, 128)
            grad = mm_tn(normed, dqkv_ref[:, pl.ds(first, 384)])
            proj = mm_tn(mixed, cot_ref[:, pl.ds(pl.multiple_of(256 * yh + 128 * owner, 128), 128)])
            tiles = [grad[:, 128 * t : 128 * t + 128] for t in range(3)] + [proj]
            for xy in range(8):
                chunk = [v[64 * xy : 64 * xy + 64].reshape(8, 8, 128) for v in tiles]
                for t in range(2):
                    piece = jnp.concatenate([chunk[2 * t], chunk[2 * t + 1]], axis=1).astype(BF)
                    out_ref[xy, :, yh, 16 * t : 16 * t + 16, :] = piece
    wide_ref[...] = mm(left_ref[...].astype(BF), spread_t[:128, :]) + mm(right_ref[...].astype(BF), spread_t[128:, :])
    blank = jnp.zeros((8, 512 - SPAN), F32)
    levels = []
    for l in range(2):
        outer = None
        for r in reversed(range(ROWS)):
            inner = None
            for c in reversed(range(COLS)):
                q = 8 * (l * 72 + r * 12 + c)
                here = jnp.concatenate([wide_ref[q : q + 8, :], blank], axis=1)
                inner = here if inner is None else pltpu.roll(inner, 1, 1) + here
            outer = inner if outer is None else pltpu.roll(outer, 23, 1) + inner
        levels.append(jnp.concatenate([outer, jnp.zeros((8, 256), F32)], axis=1))
    bias_grad = levels[0] + pltpu.roll(levels[1], 253, 1)
    for i in range(6):
        small_ref[8 * i : 8 * i + 8, :] = bias_grad[:, 128 * i : 128 * i + 128]


def attend_back(core, cot, x, qkv, p, mixed, wqkv, wproj, gain, merge_gain):
    shapes = [
        jax.ShapeDtypeStruct((TOK, 512), BF), jax.ShapeDtypeStruct((80, 128), F32),
    ] + [jax.ShapeDtypeStruct((8, 8, 2, 32, 128), BF)] * 2
    return pl.pallas_call(
        back_kernel,
        out_shape=shapes,
        in_specs=[pl.BlockSpec(memory_space=pltpu.SMEM)] + vmem(11),
        out_specs=vmem(4),
        scratch_shapes=[pltpu.VMEM((TOK, 1536), BF), pltpu.VMEM((8 * WIN, 128), F32), pltpu.VMEM((8 * WIN, 128), F32), pltpu.VMEM((8 * WIN, SPAN), F32)],
        compiler_params=PARAMS,
        cost_estimate=cost(8_000_000_000, 16_000_000),
    )(core, cot, x, qkv, p, mixed, wqkv, wproj, gain, merge_gain, plan("spread_t"), plan("back"))


def total_of(axes):
    total = 1
    for axis in axes:
        total *= lax.axis_size(axis)
    return total


def moved(block, axes, distance):
    count = total_of(axes)
    return lax.ppermute(block, axes, [((i - distance) % count, i) for i in range(count)])


def pack_kernel(mine_ref, theirs_ref, small_ref, small_theirs_ref, out_ref):
    out_ref[:, :512, :] = (mine_ref[...].astype(F32) + theirs_ref[...].astype(F32)).astype(BF)
    small = (small_ref[...] + small_theirs_ref[...]).astype(BF)
    for i in range(8):
        out_ref[i, 512:, :] = small


def pack(mine, theirs, small, small_theirs):
    return pl.pallas_call(
        pack_kernel,
        out_shape=jax.ShapeDtypeStruct((8, 592, 128), BF),
        in_specs=vmem(4),
        out_specs=vmem(1)[0],
        compiler_params=PARAMS,
    )(mine, theirs, small, small_theirs)


def pair_kernel(early_ref, out_ref):
    tokens = early_ref[...].reshape(1280, 768)
    grad = mm_tn(tokens[:, :256], tokens[:, 256:])
    for z in range(8):
        for yh in range(2):
            for t in range(2):
                piece = grad[32 * z : 32 * z + 32, 256 * yh + 128 * t : 256 * yh + 128 * t + 128]
                out_ref[2 * z + yh, 32 * t : 32 * t + 32, :] = piece.astype(BF)


def pair_grad(early):
    return pl.pallas_call(
        pair_kernel,
        out_shape=jax.ShapeDtypeStruct((16, 64, 128), BF),
        in_specs=vmem(1),
        out_specs=vmem(1)[0],
        compiler_params=PARAMS,
    )(early)


def fold_kernel(early_ref, late_ref, out_ref):
    out_ref[:, :64, :] = early_ref[...]
    late = jnp.sum(late_ref[...].astype(F32), axis=0).astype(BF)
    out_ref[:, 64:96, :] = late[:512].reshape(16, 32, 128)
    for i in range(16):
        out_ref[i, 96:, :] = late[512:]


def fold(early, late):
    return pl.pallas_call(
        fold_kernel,
        out_shape=jax.ShapeDtypeStruct((16, 176, 128), BF),
        in_specs=vmem(2),
        out_specs=vmem(1)[0],
        compiler_params=PARAMS,
    )(early, late)


def unpack_kernel(got_ref, qkv_ref, proj_ref, merge_ref, norm_gain_ref, merge_gain_ref, bias_ref):
    total = jnp.sum(got_ref[...].astype(F32), axis=0)
    for t in range(2):
        merge_ref[:, 128 * t : 128 * t + 128] = total[32 * t : 32 * t + 32]
    for t in range(3):
        qkv_ref[:, 128 * t : 128 * t + 128] = total[64 + 8 * t : 72 + 8 * t]
    proj_ref[...] = total[88:96]
    for t in range(6):
        width = min(128, TABLE - 128 * t)
        bias_ref[:, 128 * t : 128 * t + width] = total[96 + 8 * t : 104 + 8 * t, :width]
    merge_gain_ref[...] = total[144:160]
    norm_gain_ref[...] = total[160:168]


def unpack(got):
    shapes = [(8, 384), (8, 128), (32, 256), (8, 128), (16, 128), (8, TABLE)]
    return pl.pallas_call(
        unpack_kernel,
        out_shape=[jax.ShapeDtypeStruct(s, F32) for s in shapes],
        in_specs=vmem(1),
        out_specs=vmem(6),
        compiler_params=PARAMS,
    )(got)


def swapped(value, axis, bit):
    count = lax.axis_size(axis)
    return lax.ppermute(value, axis, [(i ^ bit, i) for i in range(count)])


def diagonal(block, distance):
    route = [(((i // 4 - distance) % 64) * 4 + (i % 4 - distance) % 4, i) for i in range(256)]
    return lax.ppermute(block, AXES, route)


def spread_over(parts, axes):
    return lax.all_to_all(parts, axes, 0, 0, tiled=True)


def home(field, rows, width):
    north = moved(field[rows:, :width], LAT, 1)
    east = moved(field[:rows, width:], LON, 1)
    corner = diagonal(field[rows:, width:], 1)
    top = jnp.concatenate([corner, north], axis=1)
    return jnp.concatenate([top, jnp.concatenate([east, field[:rows, :width]], axis=1)], axis=0)


def on_device(features, norm_gain, qkv_weight, proj_weight, bias_table, merge_gain, merge_weight, merged_cot):
    last = (lax.axis_index(LAT) == total_of(LAT) - 1).astype(jnp.int32).reshape(1)
    gain, wide_gain = norm_gain.reshape(1, 512), merge_gain.reshape(1, 2048)
    own = features.transpose(1, 2, 0, 3).reshape(6, 48, 512)
    cot = merged_cot.transpose(1, 2, 0, 3).reshape(3, 24, 1024)
    west = moved(own[:, :24], LON, -1)
    south = moved(own[:3, 24:], LAT, -1)
    corner = diagonal(own[:3, :24], -1)
    bias, mask = bias_of(bias_table, last)
    flat = own.reshape(TOK, 512)
    flat, bias, mask, west, south, corner = lax.optimization_barrier((flat, bias, mask, west, south, corner))
    x, qkv, p, mixed, block, first, final = attend(
        flat, west.reshape(144, 512), south.reshape(72, 512), corner.reshape(72, 512),
        gain, qkv_weight, proj_weight, bias, mask,
    )
    following = moved(first, LAT, -1)
    prev = moved(final, LAT, 1)
    cot, block = lax.optimization_barrier((cot, block))
    cot_west = moved(cot[1:, :12], LON, -1)
    cot_south = moved(cot[:2, 12:], LAT, -1)
    cot_corner = diagonal(cot[:2, :12], -1)
    core = lax.axis_index("c").astype(jnp.int32).reshape(1)
    pair, hats, scale, all_cot = stack(
        block, prev, following, cot.reshape(72, 1024), cot_west.reshape(24, 1024), cot_south.reshape(24, 1024),
        cot_corner.reshape(24, 1024), wide_gain,
    )
    early = spread_over(pair, CLOSE)
    merged, attn_cot, merge_gain_part = merge(hats, scale, all_cot, wide_gain, merge_weight)
    merged = home(merged.reshape(3, 24, 1024), 2, 12)
    grad, small, late, late_out = attend_back(
        core, attn_cot, x, qkv, p, mixed, qkv_weight, proj_weight, gain, merge_gain_part
    )

    late_theirs, small_theirs = swapped(late_out, "c", 1), swapped(small, "c", 1)
    late = pack(late.reshape(8, 512, 128), late_theirs.reshape(8, 512, 128), small, small_theirs)
    late, early = lax.optimization_barrier((late, early))
    late = spread_over(late, NEAR)
    early = pair_grad(early)
    grad = home(grad.reshape(6, 48, 512), 3, 24)
    late, early, grad, merged = lax.optimization_barrier((late, early, grad, merged))
    merged = merged.reshape(3, 6, 4, 1024).transpose(2, 0, 1, 3)
    features_grad = grad.reshape(6, 12, 4, 512).transpose(2, 0, 1, 3)
    got = spread_over(fold(early, late), FAR)
    qkv_grad, proj_grad, merge_grad, norm_gain_grad, merge_gain_grad, bias_grad = unpack(got)
    return (
        merged,
        features_grad,
        qkv_grad,
        proj_grad,
        merge_grad,
        norm_gain_grad[:4].reshape(-1),
        merge_gain_grad.reshape(-1),
        bias_grad,
    )


def solution(mesh):
    fine = Mesh(mesh.devices.reshape(4, 2, 8, 2, 2), AXES)
    field = P(None, LAT, LON, None)
    return jax.shard_map(
        on_device,
        mesh=fine,
        in_specs=(field, P(), P(), P(), P(), P(), P(), field),
        out_specs=(field, field, P(LON, LAT), P(LON, LAT), P(LON, LAT), P(), P(), P()),
        check_vma=False,
    )
```

```python
import functools

import jax
import jax.numpy as jnp
import numpy as np
from jax import lax
from jax.experimental import pallas as pl
from jax.experimental.pallas import tpu as pltpu
from jax.sharding import Mesh
from jax.sharding import PartitionSpec as P

EPSILON = 1e-05
MASKED = -1000000000.0
HEADS, LEV, ROWS, COLS = 8, 4, 6, 12
WIN = 144
TOK = 288
HALF_LON, HALF_LAT = 6, 3
SPAN = 384
TABLE = 759
AXES = ("x", "yl", "z", "yh", "c")
LON, LAT = ("x", "yl", "z"), ("yh", "c")
NEAR, FAR, CLOSE = ("x", "yl"), ("z", "yh"), ("x", "yl", "c")
BF, F32 = jnp.bfloat16, jnp.float32


def token(w, l, r, c):
    return w * WIN + l * 72 + r * 12 + c


def level_of(w, l):
    return (2 * w + l + 1) % LEV


def plans():
    own = np.zeros((TOK, TOK)); west = np.zeros((TOK, 144)); south = np.zeros((TOK, 72)); corner = np.zeros((TOK, 72))
    back = np.zeros((TOK, TOK))
    quad_own = np.zeros((4 * 96, TOK)); quad_prev = np.zeros((4 * 96, 48)); quad_next = np.zeros((4 * 96, 48))
    edge = np.zeros((96, TOK))
    for w in range(2):
        for l in range(2):
            lev, s = level_of(w, l), 2 * w + l
            for r in range(ROWS):
                for c in range(COLS):
                    t = token(w, l, r, c)
                    i, j = r + HALF_LAT, c + HALF_LON
                    if i >= ROWS and j >= COLS:
                        corner[t, ((i - ROWS) * HALF_LON + j - COLS) * LEV + lev] = 1
                    elif i >= ROWS:
                        south[t, ((i - ROWS) * HALF_LON + c) * LEV + lev] = 1
                    elif j >= COLS:
                        west[t, (i * HALF_LON + j - COLS) * LEV + lev] = 1
                    else:
                        own[t, (i * COLS + j) * LEV + lev] = 1
                    part = (r >= 3) * 1 + (c >= 6) * 2
                    back[part * 72 + ((r % 3) * 6 + c % 6) * LEV + lev, t] = 1
                    dj, pc = c % 2, c // 2
                    if r % 2:
                        di, pr = 0, (r + 1) // 2
                    else:
                        di, pr = 1, r // 2
                    quad_own[(dj * 2 + di) * 96 + pr * 24 + s * 6 + pc, t] = 1
                    if r == 0:
                        edge[s * 12 + c, t] = 1
                    if r == ROWS - 1:
                        edge[48 + s * 12 + c, t] = 1
            for c in range(COLS):
                dj, pc = c % 2, c // 2
                quad_prev[(dj * 2 + 0) * 96 + 0 * 24 + s * 6 + pc, s * 12 + c] = 1
                quad_next[(dj * 2 + 1) * 96 + 3 * 24 + s * 6 + pc, s * 12 + c] = 1
    cot_own = np.zeros((3, 96, 24)); cot_west = np.zeros((2, 96, 12)); cot_south = np.zeros((2, 96, 12)); cot_corner = np.zeros((2, 96, 12))
    coarse = np.zeros((96, 96))
    for pr in range(4):
        for s in range(LEV):
            lev = (s + 1) % LEV
            for pc in range(6):
                p = pr * 24 + s * 6 + pc
                i, j = pr + 1, pc + 3
                if i >= 3 and j >= 6:
                    cot_corner[i - 3, p, (j - 6) * LEV + lev] = 1
                elif i >= 3:
                    cot_south[i - 3, p, pc * LEV + lev] = 1
                elif j >= 6:
                    cot_west[i - 1, p, (j - 6) * LEV + lev] = 1
                else:
                    cot_own[i, p, j * LEV + lev] = 1
                if pr < 3:
                    start = (0 if pc < 3 else 32) if pr < 2 else (64 if pc < 3 else 80)
                    coarse[start + ((pr % 2) * 3 + pc % 3) * LEV + lev, p] = 1
    place = np.zeros(WIN, np.int64)
    for l in range(2):
        for r in range(ROWS):
            for c in range(COLS):
                place[l * 72 + r * 12 + c] = l * 253 + r * 23 + c
    spread = np.zeros((SPAN, 256))
    spread[379 - place, np.arange(WIN)] = 1
    level = np.arange(WIN) // 72
    north = (np.arange(WIN) % 72) // 12 >= HALF_LAT
    return dict(
        own=own, west=west, south=south, corner=corner, back=back, quad_own=quad_own, quad_prev=quad_prev,
        quad_next=quad_next, quad_t=quad_own.T, edge=edge, cot_own=cot_own, cot_west=cot_west,
        cot_south=cot_south, cot_corner=cot_corner, coarse=coarse, spread=spread, spread_t=spread.T,
        apart_level=(level[:, None] != level[None]) * 1.0,
        apart_north=(north[:, None] != north[None]) * 1.0,
    ), [int(v) for v in place]


PLAN, PLACE = plans()


def plan(name):
    return jnp.asarray(PLAN[name], BF)


def mm(a, b):
    return jnp.dot(a, b, preferred_element_type=F32)


def mm_nt(a, b):
    return lax.dot_general(a, b, (((1,), (1,)), ((), ())), preferred_element_type=F32)


def mm_tn(a, b):
    return lax.dot_general(a, b, (((0,), (0,)), ((), ())), preferred_element_type=F32)


def vmem(count):
    return [pl.BlockSpec(memory_space=pltpu.VMEM)] * count


def cost(flops, moved_bytes):
    return pl.CostEstimate(flops=flops, bytes_accessed=moved_bytes, transcendentals=0)


PARAMS = pltpu.CompilerParams(vmem_limit_bytes=56 * 1024 * 1024)


def bias_kernel(last_ref, table_ref, spread_ref, level_ref, north_ref, bias_ref, mask_ref, rows_ref, left_ref, right_ref):
    table = jnp.concatenate([table_ref[...], jnp.zeros((8, 768 - TABLE), F32)], axis=1)
    for q in range(WIN):
        rows_ref[8 * q : 8 * q + 8, :] = pltpu.roll(table, (768 - PLACE[q]) % 768, 1)[:, :SPAN]
    rows = rows_ref[...]
    high = rows.astype(BF)
    rest = rows - high.astype(F32)
    middle = rest.astype(BF)
    low = (rest - middle.astype(F32)).astype(BF)
    spread = spread_ref[...]
    wide = mm(high, spread) + mm(middle, spread) + mm(low, spread)
    left_ref[...] = wide[:, :128]
    right_ref[...] = wide[:, 128:]
    for h in range(HEADS):
        bias_ref[h, :, :128] = left_ref[pl.ds(h, WIN, stride=8), :]
        bias_ref[h, :, 128:] = right_ref[pl.ds(h, WIN, stride=8), :][:, :16]
    north = jnp.where(last_ref[0] == 1, north_ref[...].astype(F32), 0.0)
    mask_ref[0] = north * MASKED
    mask_ref[1] = jnp.maximum(north, level_ref[...].astype(F32)) * MASKED


def bias_of(table, last):
    shapes = [jax.ShapeDtypeStruct((HEADS, WIN, WIN), F32), jax.ShapeDtypeStruct((2, WIN, WIN), F32)]
    return pl.pallas_call(
        bias_kernel,
        out_shape=shapes,
        in_specs=[pl.BlockSpec(memory_space=pltpu.SMEM)] + vmem(4),
        out_specs=vmem(2),
        scratch_shapes=[pltpu.VMEM((8 * WIN, SPAN), F32)] + [pltpu.VMEM((8 * WIN, 128), F32)] * 2,
        compiler_params=PARAMS,
        cost_estimate=cost(2_000_000_000, 4_000_000),
    )(last, table, plan("spread"), plan("apart_level"), plan("apart_north"))


def norm_parts(values, width):
    mean = sum(jnp.sum(v, axis=1, keepdims=True) for v in values) * (1.0 / width)
    center = [v - mean for v in values]
    spread = sum(jnp.sum(v * v, axis=1, keepdims=True) for v in center) * (1.0 / width)
    scale = lax.rsqrt(spread + EPSILON)
    return [v * scale for v in center], scale


def norm_back(hats, scale, cots, gains, width):
    inner = [c * g for c, g in zip(cots, gains)]
    first = sum(jnp.sum(v, axis=1, keepdims=True) for v in inner) * (1.0 / width)
    second = sum(jnp.sum(v * h, axis=1, keepdims=True) for v, h in zip(inner, hats)) * (1.0 / width)
    return [scale * (v - first - h * second) for v, h in zip(inner, hats)]


def lower_half():
    return lax.broadcasted_iota(jnp.int32, (WIN, 128), 1) < 64


def attend_kernel(
    own_ref, west_ref, south_ref, corner_ref, plan_own, plan_west, plan_south, plan_corner, plan_edge, gain_ref, wqkv_ref, wproj_ref,
    bias_ref, mask_ref, x_ref, qkv_ref, p_ref, tokens_ref, block_ref, first_ref, last_ref,
):
    x = (
        mm(plan_own[...], own_ref[...]) + mm(plan_west[...], west_ref[...])
        + mm(plan_south[...], south_ref[...]) + mm(plan_corner[...], corner_ref[...])
    )
    x_ref[...] = x.astype(BF)
    (hat,), _ = norm_parts([x], 512)
    normed = (hat * gain_ref[...]).astype(BF)
    tokens_ref[:, :512] = normed
    qkv_ref[...] = mm(normed, wqkv_ref[...]).astype(BF)
    lower = lower_half()
    for w in range(2):
        rows = slice(w * WIN, (w + 1) * WIN)
        for pair in range(4):
            lanes = slice(pair * 128, pair * 128 + 128)
            query = qkv_ref[rows, lanes]
            key = qkv_ref[rows, 512 + pair * 128 : 640 + pair * 128]
            value = qkv_ref[rows, 1024 + pair * 128 : 1152 + pair * 128]
            outs = []
            for half in range(2):
                h = 2 * pair + half
                keep = lower if half == 0 else jnp.logical_not(lower)
                part = jnp.where(keep, query * 0.125, 0.0).astype(BF)
                scores = mm_nt(part, key) + bias_ref[h] + mask_ref[w]
                top = jnp.max(scores, axis=1, keepdims=True)
                grown = jnp.exp(scores - top)
                weights = (grown / jnp.sum(grown, axis=1, keepdims=True)).astype(BF)
                p_ref[w * HEADS + h] = weights
                outs.append(mm(weights, value))
            tokens_ref[rows, 512 + pair * 128 : 640 + pair * 128] = jnp.where(lower, outs[0], outs[1]).astype(BF)
    attended = mm(tokens_ref[:, 512:], wproj_ref[...]).astype(BF)
    block = (x + attended.astype(F32)).astype(BF)
    block_ref[...] = block
    edge = mm(plan_edge[...], block).astype(BF)
    first_ref[...] = edge[:48]
    last_ref[...] = edge[48:]


def attend(own, west, south, corner, gain, wqkv, wproj, bias, mask):
    shapes = [(TOK, 512), (TOK, 1536), (2 * HEADS, WIN, WIN), (TOK, 1024), (TOK, 512), (48, 512), (48, 512)]
    return pl.pallas_call(
        attend_kernel,
        out_shape=[jax.ShapeDtypeStruct(s, BF) for s in shapes],
        in_specs=vmem(14),
        out_specs=vmem(7),
        compiler_params=PARAMS,
        cost_estimate=cost(4_000_000_000, 8_000_000),
    )(own, west, south, corner, plan("own"), plan("west"), plan("south"), plan("corner"), plan("edge"), gain, wqkv, wproj, bias, mask)


def stack_kernel(
    block_ref, prev_ref, next_ref, cot_ref, cot_west_ref, cot_south_ref, cot_corner_ref, quad_own, quad_prev, quad_next,
    plan_cot, plan_cot_west, plan_cot_south, plan_cot_corner, gain_ref, pair_ref, hats_ref, scale_ref, all_cot_ref,
):
    stacked = mm(quad_own[...], block_ref[...]) + mm(quad_prev[...], prev_ref[...]) + mm(quad_next[...], next_ref[...])
    values = [stacked[96 * k : 96 * k + 96] for k in range(4)]
    hats, scale = norm_parts(values, 2048)
    scale_ref[...] = jnp.broadcast_to(scale, (96, 128))
    normed = []
    for k in range(4):
        hats_ref[k] = hats[k]
        normed.append((hats[k] * gain_ref[:, 512 * k : 512 * k + 512]).astype(BF))
    cot = sum(mm(plan_cot[i], cot_ref[i]) for i in range(1, 3))
    for some_plan, some_ref in (
        (plan_cot_west, cot_west_ref), (plan_cot_south, cot_south_ref), (plan_cot_corner, cot_corner_ref),
    ):
        cot = cot + mm(some_plan[0], some_ref[0]) + mm(some_plan[1], some_ref[1])
    all_cot_ref[...] = cot.astype(BF)
    counted = lax.broadcasted_iota(jnp.int32, (80, 1024), 0) < 72
    cot_own = jnp.where(counted, cot[:80], 0.0).astype(BF)
    for c in range(2):
        halves = [cot_own[:, 512 * yh + 256 * c : 512 * yh + 256 * c + 256] for yh in range(2)]
        for xy in range(8):
            peer = 2 * xy + c
            pair_ref[peer, :, :256] = normed[xy // 2][:80, 256 * (xy % 2) : 256 * (xy % 2) + 256]
            pair_ref[peer, :, 256:512] = halves[0]
            pair_ref[peer, :, 512:] = halves[1]


def stack(block, prev, following, cot, cot_west, cot_south, cot_corner, gain):
    shapes = [
        jax.ShapeDtypeStruct((16, 80, 768), BF), jax.ShapeDtypeStruct((4, 96, 512), F32),
        jax.ShapeDtypeStruct((96, 128), F32), jax.ShapeDtypeStruct((96, 1024), BF),
    ]
    names = ("quad_own", "quad_prev", "quad_next", "cot_own", "cot_west", "cot_south", "cot_corner")
    return pl.pallas_call(
        stack_kernel,
        out_shape=shapes,
        in_specs=vmem(15),
        out_specs=vmem(4),
        compiler_params=PARAMS,
        cost_estimate=cost(2_000_000_000, 8_000_000),
    )(block, prev, following, cot, cot_west, cot_south, cot_corner, *[plan(n) for n in names], gain)


def merge_kernel(
    hats_ref, scale_ref, all_cot_ref, quad_t, coarse, gain_ref, wmerge_ref, merged_ref, back_ref, gain_grad_ref,
):
    gains = [gain_ref[:, 512 * k : 512 * k + 512] for k in range(4)]
    hats = [hats_ref[k] for k in range(4)]
    scale = scale_ref[:, :1]
    cot_all = all_cot_ref[...]
    cots = [mm_nt(cot_all, wmerge_ref[512 * k : 512 * k + 512, :]).astype(BF).astype(F32) for k in range(4)]
    pulled = norm_back(hats, scale, cots, gains, 2048)
    back_ref[...] = mm(quad_t[...], jnp.concatenate(pulled, axis=0).astype(BF)).astype(BF)
    normed = [(h * g).astype(BF) for h, g in zip(hats, gains)]
    merged = sum(mm(normed[k], wmerge_ref[512 * k : 512 * k + 512, :]) for k in range(4)).astype(BF)
    merged_ref[...] = mm(coarse[...], merged).astype(BF)
    for k in range(4):
        summed = jnp.sum((cots[k] * hats[k])[:72], axis=0, keepdims=True)
        for i in range(4):
            gain_grad_ref[4 * k + i : 4 * k + i + 1, :] = summed[:, 128 * i : 128 * i + 128]


def merge(hats, scale, all_cot, gain, wmerge):
    shapes = [
        jax.ShapeDtypeStruct((96, 1024), BF), jax.ShapeDtypeStruct((TOK, 512), BF),
        jax.ShapeDtypeStruct((16, 128), F32),
    ]
    return pl.pallas_call(
        merge_kernel,
        out_shape=shapes,
        in_specs=vmem(7),
        out_specs=vmem(3),
        compiler_params=PARAMS,
        cost_estimate=cost(4_000_000_000, 16_000_000),
    )(hats, scale, all_cot, plan("quad_t"), plan("coarse"), gain, wmerge)


def back_kernel(
    core_ref, cot_ref, x_ref, qkv_ref, p_ref, wqkv_ref, wproj_ref, gain_ref, merged_ref, back_plan,
    stay_ref, north_ref, east_ref, corner_ref, gain_grad_ref, mine_ref, theirs_ref, left_ref, right_ref, dqkv_ref,
):
    cot = cot_ref[...]
    mixed_cot = mm_nt(cot, wproj_ref[...]).astype(BF)
    lower = lower_half()
    for pair in range(4):
        lanes = slice(pair * 128, pair * 128 + 128)
        score_cots = [0.0, 0.0]
        for w in range(2):
            rows = slice(w * WIN, (w + 1) * WIN)
            query = qkv_ref[rows, lanes]
            key = qkv_ref[rows, 512 + pair * 128 : 640 + pair * 128]
            value = qkv_ref[rows, 1024 + pair * 128 : 1152 + pair * 128]
            out_cot = mixed_cot[rows, lanes]
            found = []
            for half in range(2):
                keep = lower if half == 0 else jnp.logical_not(lower)
                part = jnp.where(keep, out_cot, 0.0).astype(BF)
                weights = p_ref[w * HEADS + 2 * pair + half]
                weight_cot = mm_nt(part, value).astype(BF).astype(F32)
                wide = weights.astype(F32)
                product = wide * weight_cot
                score_cot = product - wide * jnp.sum(product, axis=1, keepdims=True)
                score_cots[half] = score_cots[half] + score_cot
                scaled = (score_cot * 0.125).astype(BF)
                found.append((mm(scaled, key), mm_tn(scaled, query), mm_tn(weights, out_cot)))
            for n in range(3):
                both = jnp.where(lower, found[0][n], found[1][n]).astype(BF)
                dqkv_ref[rows, 512 * n + pair * 128 : 512 * n + pair * 128 + 128] = both
        for half in range(2):
            places = pl.ds(2 * pair + half, WIN, stride=8)
            left_ref[places, :] = score_cots[half][:, :128]
            right_ref[places, :] = jnp.concatenate([score_cots[half][:, 128:], jnp.zeros((WIN, 112), F32)], axis=1)
    dqkv = dqkv_ref[...]
    x = x_ref[...].astype(F32)
    (hat,), scale = norm_parts([x], 512)
    gain = gain_ref[...]
    normed_cot = mm_nt(dqkv, wqkv_ref[...]).astype(BF).astype(F32)
    gain_grad = jnp.sum(normed_cot * hat, axis=0, keepdims=True)
    for i in range(4):
        gain_grad_ref[i : i + 1, :] = gain_grad[:, 128 * i : 128 * i + 128]
    (pulled,) = norm_back([hat], scale, [normed_cot], [gain], 512)
    total = (cot.astype(F32) + pulled.astype(BF).astype(F32)).astype(BF)
    home = mm(back_plan[...], total)
    stay_ref[...] = home[:72].astype(BF)
    for out_ref, start, rows, part in ((east_ref, 32, 32, 2), (north_ref, 64, 16, 1), (corner_ref, 80, 16, 3)):
        out_ref[:rows, :] = merged_ref[start : start + rows, :512]
        out_ref[rows : 2 * rows, :] = merged_ref[start : start + rows, 512:]
        out_ref[2 * rows :, :] = home[72 * part : 72 * part + 72].astype(BF)
    core = core_ref[0]
    for out_ref, owner in ((theirs_ref, 1 - core), (mine_ref, core)):
        for yh in range(2):
            first = pl.multiple_of(768 * yh + 384 * owner, 128)
            out_ref[:, 384 * yh : 384 * yh + 384] = dqkv_ref[:, pl.ds(first, 384)]
            first = pl.multiple_of(256 * yh + 128 * owner, 128)
            out_ref[:, 768 + 128 * yh : 896 + 128 * yh] = cot_ref[:, pl.ds(first, 128)]


def attend_back(core, cot, x, qkv, p, wqkv, wproj, gain, merged):
    shapes = [
        jax.ShapeDtypeStruct((72, 512), BF), jax.ShapeDtypeStruct((104, 512), BF),
        jax.ShapeDtypeStruct((136, 512), BF), jax.ShapeDtypeStruct((104, 512), BF),
        jax.ShapeDtypeStruct((4, 128), F32),
    ] + [jax.ShapeDtypeStruct((TOK, 1024), BF)] * 2 + [jax.ShapeDtypeStruct((8 * WIN, 128), F32)] * 2
    return pl.pallas_call(
        back_kernel,
        out_shape=shapes,
        in_specs=[pl.BlockSpec(memory_space=pltpu.SMEM)] + vmem(9),
        out_specs=vmem(9),
        scratch_shapes=[pltpu.VMEM((TOK, 1536), BF)],
        compiler_params=PARAMS,
        cost_estimate=cost(6_000_000_000, 16_000_000),
    )(core, cot, x, qkv, p, wqkv, wproj, gain, merged, plan("back"))


def small_kernel(left_ref, right_ref, spread_t, merge_gain_ref, norm_gain_ref, small_ref, wide_ref):
    small_ref[48:64, :] = merge_gain_ref[...]
    small_ref[64:80, :] = jnp.zeros((16, 128), F32)
    small_ref[64:68, :] = norm_gain_ref[...]
    wide_ref[...] = mm(left_ref[...].astype(BF), spread_t[:128, :]) + mm(right_ref[...].astype(BF), spread_t[128:, :])
    blank = jnp.zeros((8, 512 - SPAN), F32)
    levels = []
    for l in range(2):
        outer = None
        for r in reversed(range(ROWS)):
            inner = None
            for c in reversed(range(COLS)):
                q = 8 * (l * 72 + r * 12 + c)
                here = jnp.concatenate([wide_ref[q : q + 8, :], blank], axis=1)
                inner = here if inner is None else pltpu.roll(inner, 1, 1) + here
            outer = inner if outer is None else pltpu.roll(outer, 23, 1) + inner
        levels.append(jnp.concatenate([outer, jnp.zeros((8, 256), F32)], axis=1))
    bias_grad = levels[0] + pltpu.roll(levels[1], 253, 1)
    for i in range(6):
        small_ref[8 * i : 8 * i + 8, :] = bias_grad[:, 128 * i : 128 * i + 128]


def small_grads(left, right, merge_gain, norm_gain):
    return pl.pallas_call(
        small_kernel,
        out_shape=jax.ShapeDtypeStruct((80, 128), F32),
        in_specs=vmem(5),
        out_specs=vmem(1)[0],
        scratch_shapes=[pltpu.VMEM((8 * WIN, SPAN), F32)],
        compiler_params=PARAMS,
        cost_estimate=cost(2_000_000_000, 4_000_000),
    )(left, right, plan("spread_t"), merge_gain, norm_gain)


def late_kernel(rows_ref, rows_theirs_ref, columns_ref, columns_theirs_ref, small_ref, small_theirs_ref, out_ref):
    normed = jnp.concatenate([rows_ref[:, :512], rows_theirs_ref[:, :512]], axis=0)
    mixed = jnp.concatenate([rows_ref[:, 512:], rows_theirs_ref[:, 512:]], axis=0)
    columns = jnp.concatenate([columns_ref[...], columns_theirs_ref[...]], axis=0)
    grad = mm_tn(normed, columns[:, :768])
    proj = mm_tn(mixed, columns[:, 768:])
    for yh in range(2):
        tiles = [grad[:, 384 * yh + 128 * t : 384 * yh + 128 * t + 128] for t in range(3)]
        tiles.append(proj[:, 128 * yh : 128 * yh + 128])
        for xy in range(8):
            chunk = [v[64 * xy : 64 * xy + 64].reshape(8, 8, 128) for v in tiles]
            for t in range(2):
                piece = jnp.concatenate([chunk[2 * t], chunk[2 * t + 1]], axis=1).astype(BF)
                for z in range(8):
                    start = 64 * z + 32 * yh + 16 * t
                    out_ref[xy, start : start + 16, :] = piece[z]
    small = (small_ref[...] + small_theirs_ref[...]).astype(BF)
    for xy in range(8):
        out_ref[xy, 512:, :] = small


def late_grads(rows, rows_theirs, columns, columns_theirs, small, small_theirs):
    return pl.pallas_call(
        late_kernel,
        out_shape=jax.ShapeDtypeStruct((8, 592, 128), BF),
        in_specs=vmem(6),
        out_specs=vmem(1)[0],
        compiler_params=PARAMS,
        cost_estimate=cost(2_000_000_000, 4_000_000),
    )(rows, rows_theirs, columns, columns_theirs, small, small_theirs)


def total_of(axes):
    total = 1
    for axis in axes:
        total *= lax.axis_size(axis)
    return total


def moved(block, axes, distance):
    count = total_of(axes)
    return lax.ppermute(block, axes, [((i - distance) % count, i) for i in range(count)])


def pair_kernel(early_ref, out_ref):
    tokens = early_ref[...].reshape(1280, 768)
    grad = mm_tn(tokens[:, :256], tokens[:, 256:])
    for z in range(8):
        for yh in range(2):
            for t in range(2):
                piece = grad[32 * z : 32 * z + 32, 256 * yh + 128 * t : 256 * yh + 128 * t + 128]
                out_ref[2 * z + yh, 32 * t : 32 * t + 32, :] = piece.astype(BF)


def pair_grad(early):
    return pl.pallas_call(
        pair_kernel,
        out_shape=jax.ShapeDtypeStruct((16, 64, 128), BF),
        in_specs=vmem(1),
        out_specs=vmem(1)[0],
        compiler_params=PARAMS,
    )(early)


def fold_kernel(early_ref, late_ref, out_ref):
    out_ref[:, :64, :] = early_ref[...]
    late = jnp.sum(late_ref[...].astype(F32), axis=0).astype(BF)
    out_ref[:, 64:96, :] = late[:512].reshape(16, 32, 128)
    for i in range(16):
        out_ref[i, 96:, :] = late[512:]


def fold(early, late):
    return pl.pallas_call(
        fold_kernel,
        out_shape=jax.ShapeDtypeStruct((16, 176, 128), BF),
        in_specs=vmem(2),
        out_specs=vmem(1)[0],
        compiler_params=PARAMS,
    )(early, late)


def unpack_kernel(got_ref, qkv_ref, proj_ref, merge_ref, norm_gain_ref, merge_gain_ref, bias_ref):
    total = jnp.sum(got_ref[...].astype(F32), axis=0)
    for t in range(2):
        merge_ref[:, 128 * t : 128 * t + 128] = total[32 * t : 32 * t + 32]
    for t in range(3):
        qkv_ref[:, 128 * t : 128 * t + 128] = total[64 + 8 * t : 72 + 8 * t]
    proj_ref[...] = total[88:96]
    for t in range(6):
        width = min(128, TABLE - 128 * t)
        bias_ref[:, 128 * t : 128 * t + width] = total[96 + 8 * t : 104 + 8 * t, :width]
    merge_gain_ref[...] = total[144:160]
    norm_gain_ref[...] = total[160:164]


def unpack(got):
    shapes = [(8, 384), (8, 128), (32, 256), (4, 128), (16, 128), (8, TABLE)]
    return pl.pallas_call(
        unpack_kernel,
        out_shape=[jax.ShapeDtypeStruct(s, F32) for s in shapes],
        in_specs=vmem(1),
        out_specs=vmem(6),
        compiler_params=PARAMS,
    )(got)


def swapped(value, axis, bit):
    count = lax.axis_size(axis)
    return lax.ppermute(value, axis, [(i ^ bit, i) for i in range(count)])


def diagonal(block, distance):
    route = [(((i // 4 - distance) % 64) * 4 + (i % 4 - distance) % 4, i) for i in range(256)]
    return lax.ppermute(block, AXES, route)


def spread_over(parts, axes):
    return lax.all_to_all(parts, axes, 0, 0, tiled=True)


def quarters(corner, north, east, stay):
    top = jnp.concatenate([corner, north], axis=1)
    return jnp.concatenate([top, jnp.concatenate([east, stay], axis=1)], axis=0)


def on_device(features, norm_gain, qkv_weight, proj_weight, bias_table, merge_gain, merge_weight, merged_cot):
    last = (lax.axis_index(LAT) == total_of(LAT) - 1).astype(jnp.int32).reshape(1)
    gain, wide_gain = norm_gain.reshape(1, 512), merge_gain.reshape(1, 2048)
    own = features.transpose(1, 2, 0, 3).reshape(6, 48, 512)
    own, merged_cot = lax.optimization_barrier((own, merged_cot))
    cot = merged_cot.transpose(1, 2, 0, 3).reshape(3, 24, 1024)
    west = moved(own[:, :24], LON, -1)
    south = moved(own[:3, 24:], LAT, -1)
    corner = diagonal(own[:3, :24], -1)
    cot_west = moved(cot[1:, :12], LON, -1)
    cot_south = moved(cot[:2, 12:], LAT, -1)
    cot_corner = diagonal(cot[:2, :12], -1)
    bias, mask = bias_of(bias_table, last)
    flat = own.reshape(TOK, 512)
    flat, bias, mask, west, south, corner = lax.optimization_barrier((flat, bias, mask, west, south, corner))
    x, qkv, p, rows, block, first, final = attend(
        flat, west.reshape(144, 512), south.reshape(72, 512), corner.reshape(72, 512),
        gain, qkv_weight, proj_weight, bias, mask,
    )
    following = moved(first, LAT, -1)
    prev = moved(final, LAT, 1)
    core = lax.axis_index("c").astype(jnp.int32).reshape(1)
    pair, hats, scale, all_cot = stack(block, prev, following, cot, cot_west, cot_south, cot_corner, wide_gain)
    early = spread_over(pair, CLOSE)
    merged, attn_cot, merge_gain_part = merge(hats, scale, all_cot, wide_gain, merge_weight)
    rows_theirs = swapped(rows, "c", 1)
    stay, north, east, corner, norm_gain_part, columns, columns_out, left, right = attend_back(
        core, attn_cot, x, qkv, p, qkv_weight, proj_weight, gain, merged
    )
    columns_theirs = swapped(columns_out, "c", 1)
    small = small_grads(left, right, merge_gain_part, norm_gain_part)
    columns_theirs, small = lax.optimization_barrier((columns_theirs, small))
    late = late_grads(rows, rows_theirs, columns, columns_theirs, small, swapped(small, "c", 1))
    late, early = lax.optimization_barrier((late, early))
    late = spread_over(late, NEAR)
    north, east, corner = moved(north, LAT, 1), moved(east, LON, 1), diagonal(corner, 1)
    north, early = lax.optimization_barrier((north, pair_grad(early)))
    late, early, north, east, corner = lax.optimization_barrier((late, early, north, east, corner))
    got = spread_over(fold(early, late), FAR)
    grad = quarters(
        corner[32:].reshape(3, 24, 512), north[32:].reshape(3, 24, 512), east[64:].reshape(3, 24, 512),
        stay.reshape(3, 24, 512),
    )

    def wide(left, right, rows):
        return jnp.concatenate([left, right], axis=1).reshape(rows, 12, 1024)

    coarse = quarters(
        wide(corner[:12], corner[16:28], 1), wide(north[:12], north[16:28], 1),
        wide(east[:24], east[32:56], 2), merged[:24].reshape(2, 12, 1024),
    )
    merged = coarse.reshape(3, 6, 4, 1024).transpose(2, 0, 1, 3)
    features_grad = grad.reshape(6, 12, 4, 512).transpose(2, 0, 1, 3)
    qkv_grad, proj_grad, merge_grad, norm_gain_grad, merge_gain_grad, bias_grad = unpack(got)
    return (
        merged,
        features_grad,
        qkv_grad,
        proj_grad,
        merge_grad,
        norm_gain_grad.reshape(-1),
        merge_gain_grad.reshape(-1),
        bias_grad,
    )


def solution(mesh):
    fine = Mesh(mesh.devices.reshape(4, 2, 8, 2, 2), AXES)
    field = P(None, LAT, LON, None)
    return jax.shard_map(
        on_device,
        mesh=fine,
        in_specs=(field, P(), P(), P(), P(), P(), P(), field),
        out_specs=(field, field, P(LON, LAT), P(LON, LAT), P(LON, LAT), P(), P(), P()),
        check_vma=False,
    )
```

```python
import functools

import jax
import jax.numpy as jnp
import numpy as np
from jax import lax
from jax.experimental import pallas as pl
from jax.experimental.pallas import tpu as pltpu
from jax.sharding import Mesh
from jax.sharding import PartitionSpec as P

EPSILON = 1e-05
MASKED = -1000000000.0
HEADS, LEV, ROWS, COLS = 8, 4, 6, 12
WIN = 144
TOK = 288
HALF_LON, HALF_LAT = 6, 3
SPAN = 384
TABLE = 759
AXES = ("x", "yl", "z", "yh", "c")
LON, LAT = ("x", "yl", "z"), ("yh", "c")
NEAR, FAR, CLOSE = ("yl", "x"), ("yh", "z"), ("x", "yl", "c")
BF, F32 = jnp.bfloat16, jnp.float32


def token(w, l, r, c):
    return w * WIN + l * 72 + r * 12 + c


def level_of(w, l):
    return (2 * w + l + 1) % LEV


def plans():
    own = np.zeros((TOK, TOK)); west = np.zeros((TOK, 144)); south = np.zeros((TOK, 72)); corner = np.zeros((TOK, 72))
    back = np.zeros((TOK, TOK))
    quad_own = np.zeros((4 * 96, TOK)); quad_prev = np.zeros((4 * 96, 48)); quad_next = np.zeros((4 * 96, 48))
    edge = np.zeros((96, TOK))
    for w in range(2):
        for l in range(2):
            lev, s = level_of(w, l), 2 * w + l
            for r in range(ROWS):
                for c in range(COLS):
                    t = token(w, l, r, c)
                    i, j = r + HALF_LAT, c + HALF_LON
                    if i >= ROWS and j >= COLS:
                        corner[t, ((i - ROWS) * HALF_LON + j - COLS) * LEV + lev] = 1
                    elif i >= ROWS:
                        south[t, ((i - ROWS) * HALF_LON + c) * LEV + lev] = 1
                    elif j >= COLS:
                        west[t, (i * HALF_LON + j - COLS) * LEV + lev] = 1
                    else:
                        own[t, (i * COLS + j) * LEV + lev] = 1
                    part = (r >= 3) * 1 + (c >= 6) * 2
                    back[part * 72 + ((r % 3) * 6 + c % 6) * LEV + lev, t] = 1
                    dj, pc = c % 2, c // 2
                    if r % 2:
                        di, pr = 0, (r + 1) // 2
                    else:
                        di, pr = 1, r // 2
                    quad_own[(dj * 2 + di) * 96 + pr * 24 + s * 6 + pc, t] = 1
                    if r == 0:
                        edge[s * 12 + c, t] = 1
                    if r == ROWS - 1:
                        edge[48 + s * 12 + c, t] = 1
            for c in range(COLS):
                dj, pc = c % 2, c // 2
                quad_prev[(dj * 2 + 0) * 96 + 0 * 24 + s * 6 + pc, s * 12 + c] = 1
                quad_next[(dj * 2 + 1) * 96 + 3 * 24 + s * 6 + pc, s * 12 + c] = 1
    cot_own = np.zeros((3, 96, 24)); cot_west = np.zeros((2, 96, 12)); cot_south = np.zeros((2, 96, 12)); cot_corner = np.zeros((2, 96, 12))
    coarse = np.zeros((96, 96))
    for pr in range(4):
        for s in range(LEV):
            lev = (s + 1) % LEV
            for pc in range(6):
                p = pr * 24 + s * 6 + pc
                i, j = pr + 1, pc + 3
                if i >= 3 and j >= 6:
                    cot_corner[i - 3, p, (j - 6) * LEV + lev] = 1
                elif i >= 3:
                    cot_south[i - 3, p, pc * LEV + lev] = 1
                elif j >= 6:
                    cot_west[i - 1, p, (j - 6) * LEV + lev] = 1
                else:
                    cot_own[i, p, j * LEV + lev] = 1
                if pr < 3:
                    start = (0 if pc < 3 else 32) if pr < 2 else (64 if pc < 3 else 80)
                    coarse[start + ((pr % 2) * 3 + pc % 3) * LEV + lev, p] = 1
    place = np.zeros(WIN, np.int64)
    for l in range(2):
        for r in range(ROWS):
            for c in range(COLS):
                place[l * 72 + r * 12 + c] = l * 253 + r * 23 + c
    spread = np.zeros((SPAN, 256))
    spread[379 - place, np.arange(WIN)] = 1
    level = np.arange(WIN) // 72
    north = (np.arange(WIN) % 72) // 12 >= HALF_LAT
    return dict(
        own=own, west=west, south=south, corner=corner, back=back, quad_own=quad_own, quad_prev=quad_prev,
        quad_next=quad_next, quad_t=quad_own.T, edge=edge, cot_own=cot_own, cot_west=cot_west,
        cot_south=cot_south, cot_corner=cot_corner, coarse=coarse, spread=spread, spread_t=spread.T,
        apart_level=(level[:, None] != level[None]) * 1.0,
        apart_north=(north[:, None] != north[None]) * 1.0,
    ), [int(v) for v in place]


PLAN, PLACE = plans()


def plan(name):
    return jnp.asarray(PLAN[name], BF)


def mm(a, b):
    return jnp.dot(a, b, preferred_element_type=F32)


def mm_nt(a, b):
    return lax.dot_general(a, b, (((1,), (1,)), ((), ())), preferred_element_type=F32)


def mm_tn(a, b):
    return lax.dot_general(a, b, (((0,), (0,)), ((), ())), preferred_element_type=F32)


def vmem(count):
    return [pl.BlockSpec(memory_space=pltpu.VMEM)] * count


def cost(flops, moved_bytes):
    return pl.CostEstimate(flops=flops, bytes_accessed=moved_bytes, transcendentals=0)


PARAMS = pltpu.CompilerParams(vmem_limit_bytes=56 * 1024 * 1024)


def bias_kernel(last_ref, table_ref, spread_ref, level_ref, north_ref, bias_ref, mask_ref, rows_ref, left_ref, right_ref):
    table = jnp.concatenate([table_ref[...], jnp.zeros((8, 768 - TABLE), F32)], axis=1)
    for q in range(WIN):
        rows_ref[8 * q : 8 * q + 8, :] = pltpu.roll(table, (768 - PLACE[q]) % 768, 1)[:, :SPAN]
    rows = rows_ref[...]
    high = rows.astype(BF)
    rest = rows - high.astype(F32)
    middle = rest.astype(BF)
    low = (rest - middle.astype(F32)).astype(BF)
    spread = spread_ref[...]
    wide = mm(high, spread) + mm(middle, spread) + mm(low, spread)
    left_ref[...] = wide[:, :128]
    right_ref[...] = wide[:, 128:]
    for h in range(HEADS):
        bias_ref[h, :, :128] = left_ref[pl.ds(h, WIN, stride=8), :]
        bias_ref[h, :, 128:] = right_ref[pl.ds(h, WIN, stride=8), :][:, :16]
    north = jnp.where(last_ref[0] == 1, north_ref[...].astype(F32), 0.0)
    mask_ref[0] = north * MASKED
    mask_ref[1] = jnp.maximum(north, level_ref[...].astype(F32)) * MASKED


def bias_of(table, last):
    shapes = [jax.ShapeDtypeStruct((HEADS, WIN, WIN), F32), jax.ShapeDtypeStruct((2, WIN, WIN), F32)]
    return pl.pallas_call(
        bias_kernel,
        out_shape=shapes,
        in_specs=[pl.BlockSpec(memory_space=pltpu.SMEM)] + vmem(4),
        out_specs=vmem(2),
        scratch_shapes=[pltpu.VMEM((8 * WIN, SPAN), F32)] + [pltpu.VMEM((8 * WIN, 128), F32)] * 2,
        compiler_params=PARAMS,
        cost_estimate=cost(2_000_000_000, 4_000_000),
    )(last, table, plan("spread"), plan("apart_level"), plan("apart_north"))


def norm_parts(values, width):
    mean = sum(jnp.sum(v, axis=1, keepdims=True) for v in values) * (1.0 / width)
    center = [v - mean for v in values]
    spread = sum(jnp.sum(v * v, axis=1, keepdims=True) for v in center) * (1.0 / width)
    scale = lax.rsqrt(spread + EPSILON)
    return [v * scale for v in center], scale


def norm_back(hats, scale, cots, gains, width):
    inner = [c * g for c, g in zip(cots, gains)]
    first = sum(jnp.sum(v, axis=1, keepdims=True) for v in inner) * (1.0 / width)
    second = sum(jnp.sum(v * h, axis=1, keepdims=True) for v, h in zip(inner, hats)) * (1.0 / width)
    return [scale * (v - first - h * second) for v, h in zip(inner, hats)]


def lower_half():
    return lax.broadcasted_iota(jnp.int32, (WIN, 128), 1) < 64


def attend_kernel(
    own_ref, west_ref, south_ref, corner_ref, plan_own, plan_west, plan_south, plan_corner, plan_edge, gain_ref, wqkv_ref, wproj_ref,
    bias_ref, mask_ref, x_ref, qkv_ref, p_ref, tokens_ref, block_ref, first_ref, last_ref,
):
    x = (
        mm(plan_own[...], own_ref[...]) + mm(plan_west[...], west_ref[...])
        + mm(plan_south[...], south_ref[...]) + mm(plan_corner[...], corner_ref[...])
    )
    x_ref[...] = x.astype(BF)
    (hat,), _ = norm_parts([x], 512)
    normed = (hat * gain_ref[...]).astype(BF)
    tokens_ref[:, :512] = normed
    qkv_ref[...] = mm(normed, wqkv_ref[...]).astype(BF)
    lower = lower_half()
    for w in range(2):
        rows = slice(w * WIN, (w + 1) * WIN)
        for pair in range(4):
            lanes = slice(pair * 128, pair * 128 + 128)
            query = qkv_ref[rows, lanes]
            key = qkv_ref[rows, 512 + pair * 128 : 640 + pair * 128]
            value = qkv_ref[rows, 1024 + pair * 128 : 1152 + pair * 128]
            outs = []
            for half in range(2):
                h = 2 * pair + half
                keep = lower if half == 0 else jnp.logical_not(lower)
                part = jnp.where(keep, query * 0.125, 0.0).astype(BF)
                scores = mm_nt(part, key) + bias_ref[h] + mask_ref[w]
                top = jnp.max(scores, axis=1, keepdims=True)
                grown = jnp.exp(scores - top)
                weights = (grown / jnp.sum(grown, axis=1, keepdims=True)).astype(BF)
                p_ref[w * HEADS + h] = weights
                outs.append(mm(weights, value))
            tokens_ref[rows, 512 + pair * 128 : 640 + pair * 128] = jnp.where(lower, outs[0], outs[1]).astype(BF)
    attended = mm(tokens_ref[:, 512:], wproj_ref[...]).astype(BF)
    block = (x + attended.astype(F32)).astype(BF)
    block_ref[...] = block
    edge = mm(plan_edge[...], block).astype(BF)
    first_ref[...] = edge[:48]
    last_ref[...] = edge[48:]


def attend(own, west, south, corner, gain, wqkv, wproj, bias, mask):
    shapes = [(TOK, 512), (TOK, 1536), (2 * HEADS, WIN, WIN), (TOK, 1024), (TOK, 512), (48, 512), (48, 512)]
    return pl.pallas_call(
        attend_kernel,
        out_shape=[jax.ShapeDtypeStruct(s, BF) for s in shapes],
        in_specs=vmem(14),
        out_specs=vmem(7),
        compiler_params=PARAMS,
        cost_estimate=cost(4_000_000_000, 8_000_000),
    )(own, west, south, corner, plan("own"), plan("west"), plan("south"), plan("corner"), plan("edge"), gain, wqkv, wproj, bias, mask)


def stack_kernel(
    block_ref, prev_ref, next_ref, cot_ref, cot_west_ref, cot_south_ref, cot_corner_ref, quad_own, quad_prev, quad_next,
    plan_cot, plan_cot_west, plan_cot_south, plan_cot_corner, gain_ref, pair_ref, hats_ref, scale_ref, all_cot_ref,
):
    stacked = mm(quad_own[...], block_ref[...]) + mm(quad_prev[...], prev_ref[...]) + mm(quad_next[...], next_ref[...])
    values = [stacked[96 * k : 96 * k + 96] for k in range(4)]
    hats, scale = norm_parts(values, 2048)
    scale_ref[...] = jnp.broadcast_to(scale, (96, 128))
    normed = []
    for k in range(4):
        hats_ref[k] = hats[k]
        normed.append((hats[k] * gain_ref[:, 512 * k : 512 * k + 512]).astype(BF))
    cot = sum(mm(plan_cot[i], cot_ref[i]) for i in range(1, 3))
    for some_plan, some_ref in (
        (plan_cot_west, cot_west_ref), (plan_cot_south, cot_south_ref), (plan_cot_corner, cot_corner_ref),
    ):
        cot = cot + mm(some_plan[0], some_ref[0]) + mm(some_plan[1], some_ref[1])
    all_cot_ref[...] = cot.astype(BF)
    counted = lax.broadcasted_iota(jnp.int32, (80, 1024), 0) < 72
    cot_own = jnp.where(counted, cot[:80], 0.0).astype(BF)
    for c in range(2):
        halves = [cot_own[:, 512 * yh + 256 * c : 512 * yh + 256 * c + 256] for yh in range(2)]
        for xy in range(8):
            peer = 2 * xy + c
            pair_ref[peer, :, :256] = normed[xy // 2][:80, 256 * (xy % 2) : 256 * (xy % 2) + 256]
            pair_ref[peer, :, 256:512] = halves[0]
            pair_ref[peer, :, 512:] = halves[1]


def stack(block, prev, following, cot, cot_west, cot_south, cot_corner, gain):
    shapes = [
        jax.ShapeDtypeStruct((16, 80, 768), BF), jax.ShapeDtypeStruct((4, 96, 512), F32),
        jax.ShapeDtypeStruct((96, 128), F32), jax.ShapeDtypeStruct((96, 1024), BF),
    ]
    names = ("quad_own", "quad_prev", "quad_next", "cot_own", "cot_west", "cot_south", "cot_corner")
    return pl.pallas_call(
        stack_kernel,
        out_shape=shapes,
        in_specs=vmem(15),
        out_specs=vmem(4),
        compiler_params=PARAMS,
        cost_estimate=cost(2_000_000_000, 8_000_000),
    )(block, prev, following, cot, cot_west, cot_south, cot_corner, *[plan(n) for n in names], gain)


def merge_kernel(
    hats_ref, scale_ref, all_cot_ref, quad_t, gain_ref, wmerge_ref, back_ref, gain_grad_ref,
):
    gains = [gain_ref[:, 512 * k : 512 * k + 512] for k in range(4)]
    hats = [hats_ref[k] for k in range(4)]
    scale = scale_ref[:, :1]
    cot_all = all_cot_ref[...]
    cots = [mm_nt(cot_all, wmerge_ref[512 * k : 512 * k + 512, :]).astype(BF).astype(F32) for k in range(4)]
    pulled = norm_back(hats, scale, cots, gains, 2048)
    back_ref[...] = mm(quad_t[...], jnp.concatenate(pulled, axis=0).astype(BF)).astype(BF)
    for k in range(4):
        summed = jnp.sum((cots[k] * hats[k])[:72], axis=0, keepdims=True)
        for i in range(4):
            gain_grad_ref[4 * k + i : 4 * k + i + 1, :] = summed[:, 128 * i : 128 * i + 128]


def merge(hats, scale, all_cot, gain, wmerge):
    shapes = [
        jax.ShapeDtypeStruct((TOK, 512), BF), jax.ShapeDtypeStruct((16, 128), F32),
    ]
    return pl.pallas_call(
        merge_kernel,
        out_shape=shapes,
        in_specs=vmem(6),
        out_specs=vmem(2),
        compiler_params=PARAMS,
        cost_estimate=cost(4_000_000_000, 16_000_000),
    )(hats, scale, all_cot, plan("quad_t"), gain, wmerge)


def back_kernel(
    core_ref, cot_ref, x_ref, qkv_ref, p_ref, wqkv_ref, wproj_ref, gain_ref, back_plan,
    home_ref, gain_grad_ref, mine_ref, theirs_ref, left_ref, right_ref, dqkv_ref,
):
    cot = cot_ref[...]
    mixed_cot = mm_nt(cot, wproj_ref[...]).astype(BF)
    lower = lower_half()
    for pair in range(4):
        lanes = slice(pair * 128, pair * 128 + 128)
        score_cots = [0.0, 0.0]
        for w in range(2):
            rows = slice(w * WIN, (w + 1) * WIN)
            query = qkv_ref[rows, lanes]
            key = qkv_ref[rows, 512 + pair * 128 : 640 + pair * 128]
            value = qkv_ref[rows, 1024 + pair * 128 : 1152 + pair * 128]
            out_cot = mixed_cot[rows, lanes]
            found = []
            for half in range(2):
                keep = lower if half == 0 else jnp.logical_not(lower)
                part = jnp.where(keep, out_cot, 0.0).astype(BF)
                weights = p_ref[w * HEADS + 2 * pair + half]
                weight_cot = mm_nt(part, value).astype(BF).astype(F32)
                wide = weights.astype(F32)
                product = wide * weight_cot
                score_cot = product - wide * jnp.sum(product, axis=1, keepdims=True)
                score_cots[half] = score_cots[half] + score_cot
                scaled = (score_cot * 0.125).astype(BF)
                found.append((mm(scaled, key), mm_tn(scaled, query), mm_tn(weights, out_cot)))
            for n in range(3):
                both = jnp.where(lower, found[0][n], found[1][n]).astype(BF)
                dqkv_ref[rows, 512 * n + pair * 128 : 512 * n + pair * 128 + 128] = both
        for half in range(2):
            places = pl.ds(2 * pair + half, WIN, stride=8)
            left_ref[places, :] = score_cots[half][:, :128]
            right_ref[places, :] = jnp.concatenate([score_cots[half][:, 128:], jnp.zeros((WIN, 112), F32)], axis=1)
    dqkv = dqkv_ref[...]
    x = x_ref[...].astype(F32)
    (hat,), scale = norm_parts([x], 512)
    gain = gain_ref[...]
    normed_cot = mm_nt(dqkv, wqkv_ref[...]).astype(BF).astype(F32)
    gain_grad = jnp.sum(normed_cot * hat, axis=0, keepdims=True)
    for i in range(4):
        gain_grad_ref[i : i + 1, :] = gain_grad[:, 128 * i : 128 * i + 128]
    (pulled,) = norm_back([hat], scale, [normed_cot], [gain], 512)
    total = (cot.astype(F32) + pulled.astype(BF).astype(F32)).astype(BF)
    home_ref[...] = mm(back_plan[...], total).astype(BF)
    core = core_ref[0]
    for out_ref, owner in ((theirs_ref, 1 - core), (mine_ref, core)):
        for yh in range(2):
            first = pl.multiple_of(768 * yh + 384 * owner, 128)
            out_ref[:, 384 * yh : 384 * yh + 384] = dqkv_ref[:, pl.ds(first, 384)]
            first = pl.multiple_of(256 * yh + 128 * owner, 128)
            out_ref[:, 768 + 128 * yh : 896 + 128 * yh] = cot_ref[:, pl.ds(first, 128)]


def attend_back(core, cot, x, qkv, p, wqkv, wproj, gain):
    shapes = [
        jax.ShapeDtypeStruct((TOK, 512), BF), jax.ShapeDtypeStruct((4, 128), F32),
    ] + [jax.ShapeDtypeStruct((TOK, 1024), BF)] * 2 + [jax.ShapeDtypeStruct((8 * WIN, 128), F32)] * 2
    return pl.pallas_call(
        back_kernel,
        out_shape=shapes,
        in_specs=[pl.BlockSpec(memory_space=pltpu.SMEM)] + vmem(8),
        out_specs=vmem(6),
        scratch_shapes=[pltpu.VMEM((TOK, 1536), BF)],
        compiler_params=PARAMS,
        cost_estimate=cost(6_000_000_000, 16_000_000),
    )(core, cot, x, qkv, p, wqkv, wproj, gain, plan("back"))


def home_kernel(
    hats_ref, gain_ref, wmerge_ref, coarse, home_ref, stay_ref, merged_ref, north_ref, east_ref, corner_ref,
):
    merged = 0.0
    for k in range(4):
        normed = (hats_ref[k] * gain_ref[:, 512 * k : 512 * k + 512]).astype(BF)
        merged = merged + mm(normed, wmerge_ref[512 * k : 512 * k + 512, :])
    merged = mm(coarse[...], merged.astype(BF))
    home = home_ref[...].astype(F32)
    stay_ref[...] = home[:72].astype(BF)
    merged_ref[...] = merged[:32].astype(BF)
    for out_ref, start, rows, part in ((east_ref, 32, 32, 2), (north_ref, 64, 16, 1), (corner_ref, 80, 16, 3)):
        out_ref[:rows, :] = merged[start : start + rows, :512].astype(BF)
        out_ref[rows : 2 * rows, :] = merged[start : start + rows, 512:].astype(BF)
        out_ref[2 * rows :, :] = home[72 * part : 72 * part + 72].astype(BF)


def home_parts(hats, gain, wmerge, home):
    shapes = [(72, 512), (32, 1024), (104, 512), (136, 512), (104, 512)]
    return pl.pallas_call(
        home_kernel,
        out_shape=[jax.ShapeDtypeStruct(s, BF) for s in shapes],
        in_specs=vmem(5),
        out_specs=vmem(5),
        compiler_params=PARAMS,
        cost_estimate=cost(1_000_000_000, 8_000_000),
    )(hats, gain, wmerge, plan("coarse"), home)


def small_kernel(left_ref, right_ref, spread_t, merge_gain_ref, norm_gain_ref, small_ref, wide_ref):
    small_ref[48:64, :] = merge_gain_ref[...]
    small_ref[64:80, :] = jnp.zeros((16, 128), F32)
    small_ref[64:68, :] = norm_gain_ref[...]
    wide_ref[...] = mm(left_ref[...].astype(BF), spread_t[:128, :]) + mm(right_ref[...].astype(BF), spread_t[128:, :])
    blank = jnp.zeros((8, 512 - SPAN), F32)
    levels = []
    for l in range(2):
        outer = None
        for r in reversed(range(ROWS)):
            inner = None
            for c in reversed(range(COLS)):
                q = 8 * (l * 72 + r * 12 + c)
                here = jnp.concatenate([wide_ref[q : q + 8, :], blank], axis=1)
                inner = here if inner is None else pltpu.roll(inner, 1, 1) + here
            outer = inner if outer is None else pltpu.roll(outer, 23, 1) + inner
        levels.append(jnp.concatenate([outer, jnp.zeros((8, 256), F32)], axis=1))
    bias_grad = levels[0] + pltpu.roll(levels[1], 253, 1)
    for i in range(6):
        small_ref[8 * i : 8 * i + 8, :] = bias_grad[:, 128 * i : 128 * i + 128]


def small_grads(left, right, merge_gain, norm_gain):
    return pl.pallas_call(
        small_kernel,
        out_shape=jax.ShapeDtypeStruct((80, 128), F32),
        in_specs=vmem(5),
        out_specs=vmem(1)[0],
        scratch_shapes=[pltpu.VMEM((8 * WIN, SPAN), F32)],
        compiler_params=PARAMS,
        cost_estimate=cost(2_000_000_000, 4_000_000),
    )(left, right, plan("spread_t"), merge_gain, norm_gain)


def late_kernel(rows_ref, rows_theirs_ref, columns_ref, columns_theirs_ref, small_ref, small_theirs_ref, out_ref):
    normed = jnp.concatenate([rows_ref[:, :512], rows_theirs_ref[:, :512]], axis=0)
    mixed = jnp.concatenate([rows_ref[:, 512:], rows_theirs_ref[:, 512:]], axis=0)
    columns = jnp.concatenate([columns_ref[...], columns_theirs_ref[...]], axis=0)
    grad = mm_tn(normed, columns[:, :768])
    proj = mm_tn(mixed, columns[:, 768:])
    for yh in range(2):
        tiles = [grad[:, 384 * yh + 128 * t : 384 * yh + 128 * t + 128] for t in range(3)]
        tiles.append(proj[:, 128 * yh : 128 * yh + 128])
        for xy in range(8):
            chunk = [v[64 * xy : 64 * xy + 64].reshape(8, 8, 128) for v in tiles]
            for t in range(2):
                piece = jnp.concatenate([chunk[2 * t], chunk[2 * t + 1]], axis=1).astype(BF)
                for z in range(8):
                    start = 256 * yh + 32 * z + 16 * t
                    out_ref[4 * (xy % 2) + xy // 2, start : start + 16, :] = piece[z]
    small = (small_ref[...] + small_theirs_ref[...]).astype(BF)
    for xy in range(8):
        out_ref[xy, 512:, :] = small


def late_grads(rows, rows_theirs, columns, columns_theirs, small, small_theirs):
    return pl.pallas_call(
        late_kernel,
        out_shape=jax.ShapeDtypeStruct((8, 592, 128), BF),
        in_specs=vmem(6),
        out_specs=vmem(1)[0],
        compiler_params=PARAMS,
        cost_estimate=cost(2_000_000_000, 4_000_000),
    )(rows, rows_theirs, columns, columns_theirs, small, small_theirs)


def total_of(axes):
    total = 1
    for axis in axes:
        total *= lax.axis_size(axis)
    return total


def moved(block, axes, distance):
    count = total_of(axes)
    return lax.ppermute(block, axes, [((i - distance) % count, i) for i in range(count)])


def pair_kernel(early_ref, out_ref):
    tokens = early_ref[...].reshape(1280, 768)
    grad = mm_tn(tokens[:, :256], tokens[:, 256:])
    for z in range(8):
        for yh in range(2):
            for t in range(2):
                piece = grad[32 * z : 32 * z + 32, 256 * yh + 128 * t : 256 * yh + 128 * t + 128]
                out_ref[8 * yh + z, 32 * t : 32 * t + 32, :] = piece.astype(BF)


def pair_grad(early):
    return pl.pallas_call(
        pair_kernel,
        out_shape=jax.ShapeDtypeStruct((16, 64, 128), BF),
        in_specs=vmem(1),
        out_specs=vmem(1)[0],
        compiler_params=PARAMS,
    )(early)


def fold_kernel(early_ref, late_ref, out_ref):
    out_ref[:, :64, :] = early_ref[...]
    late = jnp.sum(late_ref[...].astype(F32), axis=0).astype(BF)
    out_ref[:, 64:96, :] = late[:512].reshape(16, 32, 128)
    for i in range(16):
        out_ref[i, 96:, :] = late[512:]


def fold(early, late):
    return pl.pallas_call(
        fold_kernel,
        out_shape=jax.ShapeDtypeStruct((16, 176, 128), BF),
        in_specs=vmem(2),
        out_specs=vmem(1)[0],
        compiler_params=PARAMS,
    )(early, late)


def unpack_kernel(got_ref, qkv_ref, proj_ref, merge_ref, norm_gain_ref, merge_gain_ref, bias_ref):
    total = jnp.sum(got_ref[...].astype(F32), axis=0)
    for t in range(2):
        merge_ref[:, 128 * t : 128 * t + 128] = total[32 * t : 32 * t + 32]
    for t in range(3):
        qkv_ref[:, 128 * t : 128 * t + 128] = total[64 + 8 * t : 72 + 8 * t]
    proj_ref[...] = total[88:96]
    for t in range(6):
        width = min(128, TABLE - 128 * t)
        bias_ref[:, 128 * t : 128 * t + width] = total[96 + 8 * t : 104 + 8 * t, :width]
    merge_gain_ref[...] = total[144:160]
    norm_gain_ref[...] = total[160:164]


def unpack(got):
    shapes = [(8, 384), (8, 128), (32, 256), (4, 128), (16, 128), (8, TABLE)]
    return pl.pallas_call(
        unpack_kernel,
        out_shape=[jax.ShapeDtypeStruct(s, F32) for s in shapes],
        in_specs=vmem(1),
        out_specs=vmem(6),
        compiler_params=PARAMS,
    )(got)


def swapped(value, axis, bit):
    count = lax.axis_size(axis)
    return lax.ppermute(value, axis, [(i ^ bit, i) for i in range(count)])


def diagonal(block, distance):
    route = [(((i // 4 - distance) % 64) * 4 + (i % 4 - distance) % 4, i) for i in range(256)]
    return lax.ppermute(block, AXES, route)


def spread_over(parts, axes):
    return lax.all_to_all(parts, axes, 0, 0, tiled=True)


def quarters(corner, north, east, stay):
    top = jnp.concatenate([corner, north], axis=1)
    return jnp.concatenate([top, jnp.concatenate([east, stay], axis=1)], axis=0)


def on_device(features, norm_gain, qkv_weight, proj_weight, bias_table, merge_gain, merge_weight, merged_cot):
    last = (lax.axis_index(LAT) == total_of(LAT) - 1).astype(jnp.int32).reshape(1)
    gain, wide_gain = norm_gain.reshape(1, 512), merge_gain.reshape(1, 2048)
    own = features.transpose(1, 2, 0, 3).reshape(6, 48, 512)
    own, merged_cot = lax.optimization_barrier((own, merged_cot))
    cot = merged_cot.transpose(1, 2, 0, 3).reshape(3, 24, 1024)
    west = moved(own[:, :24], LON, -1)
    south = moved(own[:3, 24:], LAT, -1)
    corner = diagonal(own[:3, :24], -1)
    cot_west = moved(cot[1:, :12], LON, -1)
    cot_south = moved(cot[:2, 12:], LAT, -1)
    cot_corner = diagonal(cot[:2, :12], -1)
    bias, mask = bias_of(bias_table, last)
    flat = own.reshape(TOK, 512)
    flat, bias, mask, west, south, corner = lax.optimization_barrier((flat, bias, mask, west, south, corner))
    x, qkv, p, rows, block, first, final = attend(
        flat, west.reshape(144, 512), south.reshape(72, 512), corner.reshape(72, 512),
        gain, qkv_weight, proj_weight, bias, mask,
    )
    following = moved(first, LAT, -1)
    prev = moved(final, LAT, 1)
    core = lax.axis_index("c").astype(jnp.int32).reshape(1)
    pair, hats, scale, all_cot = stack(block, prev, following, cot, cot_west, cot_south, cot_corner, wide_gain)
    early = spread_over(pair, CLOSE)
    attn_cot, merge_gain_part = merge(hats, scale, all_cot, wide_gain, merge_weight)
    rows_theirs = swapped(rows, "c", 1)
    home, norm_gain_part, columns, columns_out, left, right = attend_back(
        core, attn_cot, x, qkv, p, qkv_weight, proj_weight, gain
    )
    columns_theirs = swapped(columns_out, "c", 1)
    small = small_grads(left, right, merge_gain_part, norm_gain_part)
    columns_theirs, small = lax.optimization_barrier((columns_theirs, small))
    late = late_grads(rows, rows_theirs, columns, columns_theirs, small, swapped(small, "c", 1))
    late, early, home = lax.optimization_barrier((late, early, home))
    late = spread_over(late, NEAR)
    stay, merged, north, east, corner = home_parts(hats, wide_gain, merge_weight, home)
    north, east, corner = moved(north, LAT, 1), moved(east, LON, 1), diagonal(corner, 1)
    last = fold(pair_grad(early), late)
    last, north, east, corner = lax.optimization_barrier((last, north, east, corner))
    got = spread_over(last, FAR)
    grad = quarters(
        corner[32:].reshape(3, 24, 512), north[32:].reshape(3, 24, 512), east[64:].reshape(3, 24, 512),
        stay.reshape(3, 24, 512),
    )

    def wide(left, right, rows):
        return jnp.concatenate([left, right], axis=1).reshape(rows, 12, 1024)

    coarse = quarters(
        wide(corner[:12], corner[16:28], 1), wide(north[:12], north[16:28], 1),
        wide(east[:24], east[32:56], 2), merged[:24].reshape(2, 12, 1024),
    )
    merged = coarse.reshape(3, 6, 4, 1024).transpose(2, 0, 1, 3)
    features_grad = grad.reshape(6, 12, 4, 512).transpose(2, 0, 1, 3)
    qkv_grad, proj_grad, merge_grad, norm_gain_grad, merge_gain_grad, bias_grad = unpack(got)
    return (
        merged,
        features_grad,
        qkv_grad,
        proj_grad,
        merge_grad,
        norm_gain_grad.reshape(-1),
        merge_gain_grad.reshape(-1),
        bias_grad,
    )


def solution(mesh):
    fine = Mesh(mesh.devices.reshape(4, 2, 8, 2, 2), AXES)
    field = P(None, LAT, LON, None)
    return jax.shard_map(
        on_device,
        mesh=fine,
        in_specs=(field, P(), P(), P(), P(), P(), P(), field),
        out_specs=(field, field, P(LON, LAT), P(LON, LAT), P(LON, LAT), P(), P(), P()),
        check_vma=False,
    )
```

```python
import functools

import jax
import jax.numpy as jnp
import numpy as np
from jax import lax
from jax.experimental import pallas as pl
from jax.experimental.pallas import tpu as pltpu
from jax.sharding import Mesh
from jax.sharding import PartitionSpec as P

EPSILON = 1e-05
MASKED = -1000000000.0
HEADS, LEV, ROWS, COLS = 8, 4, 6, 12
WIN = 144
TOK = 288
HALF_LON, HALF_LAT = 6, 3
SPAN = 384
TABLE = 759
AXES = ("x", "yl", "z", "yh", "c")
LON, LAT = ("x", "yl", "z"), ("yh", "c")
NEAR, FAR, CLOSE = ("yl", "x"), ("yh", "z"), ("x", "yl", "c")
BF, F32 = jnp.bfloat16, jnp.float32


def token(w, l, r, c):
    return w * WIN + l * 72 + r * 12 + c


def level_of(w, l):
    return (2 * w + l + 1) % LEV


def plans():
    own = np.zeros((TOK, TOK)); west = np.zeros((TOK, 144)); south = np.zeros((TOK, 72)); corner = np.zeros((TOK, 72))
    back = np.zeros((TOK, TOK))
    quad_own = np.zeros((4 * 96, TOK)); quad_prev = np.zeros((4 * 96, 48)); quad_next = np.zeros((4 * 96, 48))
    edge = np.zeros((96, TOK))
    for w in range(2):
        for l in range(2):
            lev, s = level_of(w, l), 2 * w + l
            for r in range(ROWS):
                for c in range(COLS):
                    t = token(w, l, r, c)
                    i, j = r + HALF_LAT, c + HALF_LON
                    if i >= ROWS and j >= COLS:
                        corner[t, ((i - ROWS) * HALF_LON + j - COLS) * LEV + lev] = 1
                    elif i >= ROWS:
                        south[t, ((i - ROWS) * HALF_LON + c) * LEV + lev] = 1
                    elif j >= COLS:
                        west[t, (i * HALF_LON + j - COLS) * LEV + lev] = 1
                    else:
                        own[t, (i * COLS + j) * LEV + lev] = 1
                    part = (r >= 3) * 1 + (c >= 6) * 2
                    back[part * 72 + ((r % 3) * 6 + c % 6) * LEV + lev, t] = 1
                    dj, pc = c % 2, c // 2
                    if r % 2:
                        di, pr = 0, (r + 1) // 2
                    else:
                        di, pr = 1, r // 2
                    quad_own[(dj * 2 + di) * 96 + pr * 24 + s * 6 + pc, t] = 1
                    if r == 0:
                        edge[s * 12 + c, t] = 1
                    if r == ROWS - 1:
                        edge[48 + s * 12 + c, t] = 1
            for c in range(COLS):
                dj, pc = c % 2, c // 2
                quad_prev[(dj * 2 + 0) * 96 + 0 * 24 + s * 6 + pc, s * 12 + c] = 1
                quad_next[(dj * 2 + 1) * 96 + 3 * 24 + s * 6 + pc, s * 12 + c] = 1
    cot_own = np.zeros((3, 96, 24)); cot_west = np.zeros((2, 96, 12)); cot_south = np.zeros((2, 96, 12)); cot_corner = np.zeros((2, 96, 12))
    coarse = np.zeros((96, 96))
    for pr in range(4):
        for s in range(LEV):
            lev = (s + 1) % LEV
            for pc in range(6):
                p = pr * 24 + s * 6 + pc
                i, j = pr + 1, pc + 3
                if i >= 3 and j >= 6:
                    cot_corner[i - 3, p, (j - 6) * LEV + lev] = 1
                elif i >= 3:
                    cot_south[i - 3, p, pc * LEV + lev] = 1
                elif j >= 6:
                    cot_west[i - 1, p, (j - 6) * LEV + lev] = 1
                else:
                    cot_own[i, p, j * LEV + lev] = 1
                if pr < 3:
                    start = (0 if pc < 3 else 32) if pr < 2 else (64 if pc < 3 else 80)
                    coarse[start + ((pr % 2) * 3 + pc % 3) * LEV + lev, p] = 1
    place = np.zeros(WIN, np.int64)
    for l in range(2):
        for r in range(ROWS):
            for c in range(COLS):
                place[l * 72 + r * 12 + c] = l * 253 + r * 23 + c
    spread = np.zeros((SPAN, 256))
    spread[379 - place, np.arange(WIN)] = 1
    level = np.arange(WIN) // 72
    north = (np.arange(WIN) % 72) // 12 >= HALF_LAT
    return dict(
        own=own, west=west, south=south, corner=corner, back=back, quad_own=quad_own, quad_prev=quad_prev,
        quad_next=quad_next, quad_t=quad_own.T, edge=edge, cot_own=cot_own, cot_west=cot_west,
        cot_south=cot_south, cot_corner=cot_corner, coarse=coarse, spread=spread, spread_t=spread.T,
        apart_level=(level[:, None] != level[None]) * 1.0,
        apart_north=(north[:, None] != north[None]) * 1.0,
    ), [int(v) for v in place]


PLAN, PLACE = plans()


def plan(name):
    return jnp.asarray(PLAN[name], BF)


def mm(a, b):
    return jnp.dot(a, b, preferred_element_type=F32)


def mm_nt(a, b):
    return lax.dot_general(a, b, (((1,), (1,)), ((), ())), preferred_element_type=F32)


def mm_tn(a, b):
    return lax.dot_general(a, b, (((0,), (0,)), ((), ())), preferred_element_type=F32)


def vmem(count):
    return [pl.BlockSpec(memory_space=pltpu.VMEM)] * count


def cost(flops, moved_bytes):
    return pl.CostEstimate(flops=flops, bytes_accessed=moved_bytes, transcendentals=0)


PARAMS = pltpu.CompilerParams(vmem_limit_bytes=56 * 1024 * 1024)


def bias_kernel(last_ref, table_ref, spread_ref, level_ref, north_ref, bias_ref, mask_ref, rows_ref, left_ref, right_ref):
    table = jnp.concatenate([table_ref[...], jnp.zeros((8, 768 - TABLE), F32)], axis=1)
    for q in range(WIN):
        rows_ref[8 * q : 8 * q + 8, :] = pltpu.roll(table, (768 - PLACE[q]) % 768, 1)[:, :SPAN]
    rows = rows_ref[...]
    high = rows.astype(BF)
    rest = rows - high.astype(F32)
    middle = rest.astype(BF)
    low = (rest - middle.astype(F32)).astype(BF)
    spread = spread_ref[...]
    wide = mm(high, spread) + mm(middle, spread) + mm(low, spread)
    left_ref[: 8 * WIN, :] = wide[:, :128]
    right_ref[: 8 * WIN, :] = wide[:, 128:]
    for h in range(HEADS):
        bias_ref[h, :, :128] = left_ref[pl.ds(h, WIN, stride=8), :]
        bias_ref[h, :, 128:] = right_ref[pl.ds(h, WIN, stride=8), :][:, :16]
    north = jnp.where(last_ref[0] == 1, north_ref[...].astype(F32), 0.0)
    mask_ref[0] = north * MASKED
    mask_ref[1] = jnp.maximum(north, level_ref[...].astype(F32)) * MASKED


def bias_of(table, last):
    shapes = [jax.ShapeDtypeStruct((HEADS, WIN, WIN), F32), jax.ShapeDtypeStruct((2, WIN, WIN), F32)]
    return pl.pallas_call(
        bias_kernel,
        out_shape=shapes,
        in_specs=[pl.BlockSpec(memory_space=pltpu.SMEM)] + vmem(4),
        out_specs=vmem(2),
        scratch_shapes=[pltpu.VMEM((8 * WIN, SPAN), F32)] + [pltpu.VMEM((8 * WIN + 8, 128), F32)] * 2,
        compiler_params=PARAMS,
        cost_estimate=cost(2_000_000_000, 4_000_000),
    )(last, table, plan("spread"), plan("apart_level"), plan("apart_north"))


def norm_parts(values, width):
    mean = sum(jnp.sum(v, axis=1, keepdims=True) for v in values) * (1.0 / width)
    center = [v - mean for v in values]
    spread = sum(jnp.sum(v * v, axis=1, keepdims=True) for v in center) * (1.0 / width)
    scale = lax.rsqrt(spread + EPSILON)
    return [v * scale for v in center], scale


def norm_back(hats, scale, cots, gains, width):
    inner = [c * g for c, g in zip(cots, gains)]
    first = sum(jnp.sum(v, axis=1, keepdims=True) for v in inner) * (1.0 / width)
    second = sum(jnp.sum(v * h, axis=1, keepdims=True) for v, h in zip(inner, hats)) * (1.0 / width)
    return [scale * (v - first - h * second) for v, h in zip(inner, hats)]


def lower_half():
    return lax.broadcasted_iota(jnp.int32, (WIN, 128), 1) < 64


def attend_kernel(
    own_ref, west_ref, south_ref, corner_ref, plan_own, plan_west, plan_south, plan_corner, plan_edge, gain_ref, wqkv_ref, wproj_ref,
    bias_ref, mask_ref, x_ref, qkv_ref, p_ref, tokens_ref, block_ref, first_ref, last_ref,
):
    x = (
        mm(plan_own[...], own_ref[...]) + mm(plan_west[...], west_ref[...])
        + mm(plan_south[...], south_ref[...]) + mm(plan_corner[...], corner_ref[...])
    )
    x_ref[...] = x.astype(BF)
    (hat,), _ = norm_parts([x], 512)
    normed = (hat * gain_ref[...]).astype(BF)
    tokens_ref[:, :512] = normed
    qkv_ref[...] = mm(normed, wqkv_ref[...]).astype(BF)
    lower = lower_half()
    for w in range(2):
        rows = slice(w * WIN, (w + 1) * WIN)
        for pair in range(4):
            lanes = slice(pair * 128, pair * 128 + 128)
            query = qkv_ref[rows, lanes]
            key = qkv_ref[rows, 512 + pair * 128 : 640 + pair * 128]
            value = qkv_ref[rows, 1024 + pair * 128 : 1152 + pair * 128]
            outs = []
            for half in range(2):
                h = 2 * pair + half
                keep = lower if half == 0 else jnp.logical_not(lower)
                part = jnp.where(keep, query * 0.125, 0.0).astype(BF)
                scores = mm_nt(part, key) + bias_ref[h] + mask_ref[w]
                top = jnp.max(scores, axis=1, keepdims=True)
                grown = jnp.exp(scores - top)
                weights = (grown / jnp.sum(grown, axis=1, keepdims=True)).astype(BF)
                p_ref[w * HEADS + h] = weights
                outs.append(mm(weights, value))
            tokens_ref[rows, 512 + pair * 128 : 640 + pair * 128] = jnp.where(lower, outs[0], outs[1]).astype(BF)
    attended = mm(tokens_ref[:, 512:], wproj_ref[...]).astype(BF)
    block = (x + attended.astype(F32)).astype(BF)
    block_ref[...] = block
    edge = mm(plan_edge[...], block).astype(BF)
    first_ref[...] = edge[:48]
    last_ref[...] = edge[48:]


def attend(own, west, south, corner, gain, wqkv, wproj, bias, mask):
    shapes = [(TOK, 512), (TOK, 1536), (2 * HEADS, WIN, WIN), (TOK, 1024), (TOK, 512), (48, 512), (48, 512)]
    return pl.pallas_call(
        attend_kernel,
        out_shape=[jax.ShapeDtypeStruct(s, BF) for s in shapes],
        in_specs=vmem(14),
        out_specs=vmem(7),
        compiler_params=PARAMS,
        cost_estimate=cost(4_000_000_000, 8_000_000),
    )(own, west, south, corner, plan("own"), plan("west"), plan("south"), plan("corner"), plan("edge"), gain, wqkv, wproj, bias, mask)


def stack_kernel(
    block_ref, prev_ref, next_ref, cot_ref, cot_west_ref, cot_south_ref, cot_corner_ref, quad_own, quad_prev, quad_next,
    plan_cot, plan_cot_west, plan_cot_south, plan_cot_corner, gain_ref, pair_ref, hats_ref, scale_ref, all_cot_ref,
):
    stacked = mm(quad_own[...], block_ref[...]) + mm(quad_prev[...], prev_ref[...]) + mm(quad_next[...], next_ref[...])
    values = [stacked[96 * k : 96 * k + 96] for k in range(4)]
    hats, scale = norm_parts(values, 2048)
    scale_ref[...] = jnp.broadcast_to(scale, (96, 128))
    normed = []
    for k in range(4):
        hats_ref[k] = hats[k]
        normed.append((hats[k] * gain_ref[:, 512 * k : 512 * k + 512]).astype(BF))
    cot = sum(mm(plan_cot[i], cot_ref[i]) for i in range(1, 3))
    for some_plan, some_ref in (
        (plan_cot_west, cot_west_ref), (plan_cot_south, cot_south_ref), (plan_cot_corner, cot_corner_ref),
    ):
        cot = cot + mm(some_plan[0], some_ref[0]) + mm(some_plan[1], some_ref[1])
    all_cot_ref[...] = cot.astype(BF)
    counted = lax.broadcasted_iota(jnp.int32, (80, 1024), 0) < 72
    cot_own = jnp.where(counted, cot[:80], 0.0).astype(BF)
    for c in range(2):
        halves = [cot_own[:, 512 * yh + 256 * c : 512 * yh + 256 * c + 256] for yh in range(2)]
        for xy in range(8):
            peer = 2 * xy + c
            pair_ref[peer, :, :256] = normed[xy // 2][:80, 256 * (xy % 2) : 256 * (xy % 2) + 256]
            pair_ref[peer, :, 256:512] = halves[0]
            pair_ref[peer, :, 512:] = halves[1]


def stack(block, prev, following, cot, cot_west, cot_south, cot_corner, gain):
    shapes = [
        jax.ShapeDtypeStruct((16, 80, 768), BF), jax.ShapeDtypeStruct((4, 96, 512), F32),
        jax.ShapeDtypeStruct((96, 128), F32), jax.ShapeDtypeStruct((96, 1024), BF),
    ]
    names = ("quad_own", "quad_prev", "quad_next", "cot_own", "cot_west", "cot_south", "cot_corner")
    return pl.pallas_call(
        stack_kernel,
        out_shape=shapes,
        in_specs=vmem(15),
        out_specs=vmem(4),
        compiler_params=PARAMS,
        cost_estimate=cost(2_000_000_000, 8_000_000),
    )(block, prev, following, cot, cot_west, cot_south, cot_corner, *[plan(n) for n in names], gain)


def merge_kernel(
    hats_ref, scale_ref, all_cot_ref, quad_t, gain_ref, wmerge_ref, back_ref, gain_grad_ref,
):
    gains = [gain_ref[:, 512 * k : 512 * k + 512] for k in range(4)]
    hats = [hats_ref[k] for k in range(4)]
    scale = scale_ref[:, :1]
    cot_all = all_cot_ref[...]
    cots = [mm_nt(cot_all, wmerge_ref[512 * k : 512 * k + 512, :]).astype(BF).astype(F32) for k in range(4)]
    pulled = norm_back(hats, scale, cots, gains, 2048)
    back_ref[...] = mm(quad_t[...], jnp.concatenate(pulled, axis=0).astype(BF)).astype(BF)
    for k in range(4):
        summed = jnp.sum((cots[k] * hats[k])[:72], axis=0, keepdims=True)
        for i in range(4):
            gain_grad_ref[4 * k + i : 4 * k + i + 1, :] = summed[:, 128 * i : 128 * i + 128]


def merge(hats, scale, all_cot, gain, wmerge):
    shapes = [
        jax.ShapeDtypeStruct((TOK, 512), BF), jax.ShapeDtypeStruct((16, 128), F32),
    ]
    return pl.pallas_call(
        merge_kernel,
        out_shape=shapes,
        in_specs=vmem(6),
        out_specs=vmem(2),
        compiler_params=PARAMS,
        cost_estimate=cost(4_000_000_000, 16_000_000),
    )(hats, scale, all_cot, plan("quad_t"), gain, wmerge)


def back_kernel(
    core_ref, cot_ref, x_ref, qkv_ref, p_ref, wqkv_ref, wproj_ref, gain_ref, back_plan,
    home_ref, gain_grad_ref, mine_ref, theirs_ref, left_ref, right_ref, dqkv_ref,
):
    cot = cot_ref[...]
    mixed_cot = mm_nt(cot, wproj_ref[...]).astype(BF)
    lower = lower_half()
    for pair in range(4):
        lanes = slice(pair * 128, pair * 128 + 128)
        score_cots = [0.0, 0.0]
        for w in range(2):
            rows = slice(w * WIN, (w + 1) * WIN)
            query = qkv_ref[rows, lanes]
            key = qkv_ref[rows, 512 + pair * 128 : 640 + pair * 128]
            value = qkv_ref[rows, 1024 + pair * 128 : 1152 + pair * 128]
            out_cot = mixed_cot[rows, lanes]
            found = []
            for half in range(2):
                keep = lower if half == 0 else jnp.logical_not(lower)
                part = jnp.where(keep, out_cot, 0.0).astype(BF)
                weights = p_ref[w * HEADS + 2 * pair + half]
                weight_cot = mm_nt(part, value).astype(BF).astype(F32)
                wide = weights.astype(F32)
                product = wide * weight_cot
                score_cot = product - wide * jnp.sum(product, axis=1, keepdims=True)
                score_cots[half] = score_cots[half] + score_cot
                scaled = (score_cot * 0.125).astype(BF)
                found.append((mm(scaled, key), mm_tn(scaled, query), mm_tn(weights, out_cot)))
            for n in range(3):
                both = jnp.where(lower, found[0][n], found[1][n]).astype(BF)
                dqkv_ref[rows, 512 * n + pair * 128 : 512 * n + pair * 128 + 128] = both
        for half in range(2):
            places = pl.ds(2 * pair + half, WIN, stride=8)
            left_ref[places, :] = score_cots[half][:, :128]
            right_ref[places, :] = jnp.concatenate([score_cots[half][:, 128:], jnp.zeros((WIN, 112), F32)], axis=1)
    dqkv = dqkv_ref[...]
    x = x_ref[...].astype(F32)
    (hat,), scale = norm_parts([x], 512)
    gain = gain_ref[...]
    normed_cot = mm_nt(dqkv, wqkv_ref[...]).astype(BF).astype(F32)
    gain_grad = jnp.sum(normed_cot * hat, axis=0, keepdims=True)
    for i in range(4):
        gain_grad_ref[i : i + 1, :] = gain_grad[:, 128 * i : 128 * i + 128]
    (pulled,) = norm_back([hat], scale, [normed_cot], [gain], 512)
    total = (cot.astype(F32) + pulled.astype(BF).astype(F32)).astype(BF)
    home_ref[...] = mm(back_plan[...], total).astype(BF)
    core = core_ref[0]
    for out_ref, owner in ((theirs_ref, 1 - core), (mine_ref, core)):
        for yh in range(2):
            first = pl.multiple_of(768 * yh + 384 * owner, 128)
            out_ref[:, 384 * yh : 384 * yh + 384] = dqkv_ref[:, pl.ds(first, 384)]
            first = pl.multiple_of(256 * yh + 128 * owner, 128)
            out_ref[:, 768 + 128 * yh : 896 + 128 * yh] = cot_ref[:, pl.ds(first, 128)]


def attend_back(core, cot, x, qkv, p, wqkv, wproj, gain):
    shapes = [
        jax.ShapeDtypeStruct((TOK, 512), BF), jax.ShapeDtypeStruct((4, 128), F32),
    ] + [jax.ShapeDtypeStruct((TOK, 1024), BF)] * 2 + [jax.ShapeDtypeStruct((8 * WIN + 8, 128), F32)] * 2
    return pl.pallas_call(
        back_kernel,
        out_shape=shapes,
        in_specs=[pl.BlockSpec(memory_space=pltpu.SMEM)] + vmem(8),
        out_specs=vmem(6),
        scratch_shapes=[pltpu.VMEM((TOK, 1536), BF)],
        compiler_params=PARAMS,
        cost_estimate=cost(6_000_000_000, 16_000_000),
    )(core, cot, x, qkv, p, wqkv, wproj, gain, plan("back"))


def home_kernel(
    hats_ref, gain_ref, wmerge_ref, coarse, home_ref, stay_ref, merged_ref, north_ref, east_ref, corner_ref,
):
    merged = 0.0
    for k in range(4):
        normed = (hats_ref[k] * gain_ref[:, 512 * k : 512 * k + 512]).astype(BF)
        merged = merged + mm(normed, wmerge_ref[512 * k : 512 * k + 512, :])
    merged = mm(coarse[...], merged.astype(BF))
    home = home_ref[...].astype(F32)
    stay_ref[...] = home[:72].astype(BF)
    merged_ref[...] = merged[:32].astype(BF)
    for out_ref, start, rows, part in ((east_ref, 32, 32, 2), (north_ref, 64, 16, 1), (corner_ref, 80, 16, 3)):
        out_ref[:rows, :] = merged[start : start + rows, :512].astype(BF)
        out_ref[rows : 2 * rows, :] = merged[start : start + rows, 512:].astype(BF)
        out_ref[2 * rows :, :] = home[72 * part : 72 * part + 72].astype(BF)


def home_parts(hats, gain, wmerge, home):
    shapes = [(72, 512), (32, 1024), (104, 512), (136, 512), (104, 512)]
    return pl.pallas_call(
        home_kernel,
        out_shape=[jax.ShapeDtypeStruct(s, BF) for s in shapes],
        in_specs=vmem(5),
        out_specs=vmem(5),
        compiler_params=PARAMS,
        cost_estimate=cost(1_000_000_000, 8_000_000),
    )(hats, gain, wmerge, plan("coarse"), home)


def small_kernel(left_ref, right_ref, spread_t, merge_gain_ref, norm_gain_ref, small_ref, wide_ref):
    small_ref[48:64, :] = merge_gain_ref[...]
    small_ref[64:80, :] = jnp.zeros((16, 128), F32)
    small_ref[64:68, :] = norm_gain_ref[...]
    left, right = left_ref[: 8 * WIN, :].astype(BF), right_ref[: 8 * WIN, :].astype(BF)
    wide_ref[...] = mm(left, spread_t[:128, :]) + mm(right, spread_t[128:, :])
    blank = jnp.zeros((8, 512 - SPAN), F32)
    levels = []
    for l in range(2):
        outer = None
        for r in reversed(range(ROWS)):
            inner = None
            for c in reversed(range(COLS)):
                q = 8 * (l * 72 + r * 12 + c)
                here = jnp.concatenate([wide_ref[q : q + 8, :], blank], axis=1)
                inner = here if inner is None else pltpu.roll(inner, 1, 1) + here
            outer = inner if outer is None else pltpu.roll(outer, 23, 1) + inner
        levels.append(jnp.concatenate([outer, jnp.zeros((8, 256), F32)], axis=1))
    bias_grad = levels[0] + pltpu.roll(levels[1], 253, 1)
    for i in range(6):
        small_ref[8 * i : 8 * i + 8, :] = bias_grad[:, 128 * i : 128 * i + 128]


def small_grads(left, right, merge_gain, norm_gain):
    return pl.pallas_call(
        small_kernel,
        out_shape=jax.ShapeDtypeStruct((80, 128), F32),
        in_specs=vmem(5),
        out_specs=vmem(1)[0],
        scratch_shapes=[pltpu.VMEM((8 * WIN, SPAN), F32)],
        compiler_params=PARAMS,
        cost_estimate=cost(2_000_000_000, 4_000_000),
    )(left, right, plan("spread_t"), merge_gain, norm_gain)


def late_kernel(rows_ref, rows_theirs_ref, columns_ref, columns_theirs_ref, small_ref, small_theirs_ref, out_ref):
    normed = jnp.concatenate([rows_ref[:, :512], rows_theirs_ref[:, :512]], axis=0)
    mixed = jnp.concatenate([rows_ref[:, 512:], rows_theirs_ref[:, 512:]], axis=0)
    columns = jnp.concatenate([columns_ref[...], columns_theirs_ref[...]], axis=0)
    grad = mm_tn(normed, columns[:, :768])
    proj = mm_tn(mixed, columns[:, 768:])
    for yh in range(2):
        tiles = [grad[:, 384 * yh + 128 * t : 384 * yh + 128 * t + 128] for t in range(3)]
        tiles.append(proj[:, 128 * yh : 128 * yh + 128])
        for xy in range(8):
            chunk = [v[64 * xy : 64 * xy + 64].reshape(8, 8, 128) for v in tiles]
            for t in range(2):
                piece = jnp.concatenate([chunk[2 * t], chunk[2 * t + 1]], axis=1).astype(BF)
                for z in range(8):
                    start = 256 * yh + 32 * z + 16 * t
                    out_ref[4 * (xy % 2) + xy // 2, start : start + 16, :] = piece[z]
    small = (small_ref[...] + small_theirs_ref[...]).astype(BF)
    for xy in range(8):
        out_ref[xy, 512:, :] = small


def late_grads(rows, rows_theirs, columns, columns_theirs, small, small_theirs):
    return pl.pallas_call(
        late_kernel,
        out_shape=jax.ShapeDtypeStruct((8, 592, 128), BF),
        in_specs=vmem(6),
        out_specs=vmem(1)[0],
        compiler_params=PARAMS,
        cost_estimate=cost(2_000_000_000, 4_000_000),
    )(rows, rows_theirs, columns, columns_theirs, small, small_theirs)


def total_of(axes):
    total = 1
    for axis in axes:
        total *= lax.axis_size(axis)
    return total


def moved(block, axes, distance):
    count = total_of(axes)
    return lax.ppermute(block, axes, [((i - distance) % count, i) for i in range(count)])


def pair_kernel(early_ref, out_ref):
    tokens = early_ref[...].reshape(1280, 768)
    grad = mm_tn(tokens[:, :256], tokens[:, 256:])
    for z in range(8):
        for yh in range(2):
            for t in range(2):
                piece = grad[32 * z : 32 * z + 32, 256 * yh + 128 * t : 256 * yh + 128 * t + 128]
                out_ref[8 * yh + z, 32 * t : 32 * t + 32, :] = piece.astype(BF)


def pair_grad(early):
    return pl.pallas_call(
        pair_kernel,
        out_shape=jax.ShapeDtypeStruct((16, 64, 128), BF),
        in_specs=vmem(1),
        out_specs=vmem(1)[0],
        compiler_params=PARAMS,
    )(early)


def fold_kernel(early_ref, late_ref, out_ref):
    out_ref[:, :64, :] = early_ref[...]
    late = jnp.sum(late_ref[...].astype(F32), axis=0).astype(BF)
    out_ref[:, 64:96, :] = late[:512].reshape(16, 32, 128)
    for i in range(16):
        out_ref[i, 96:, :] = late[512:]


def fold(early, late):
    return pl.pallas_call(
        fold_kernel,
        out_shape=jax.ShapeDtypeStruct((16, 176, 128), BF),
        in_specs=vmem(2),
        out_specs=vmem(1)[0],
        compiler_params=PARAMS,
    )(early, late)


def unpack_kernel(got_ref, qkv_ref, proj_ref, merge_ref, norm_gain_ref, merge_gain_ref, bias_ref):
    total = jnp.sum(got_ref[...].astype(F32), axis=0)
    for t in range(2):
        merge_ref[:, 128 * t : 128 * t + 128] = total[32 * t : 32 * t + 32]
    for t in range(3):
        qkv_ref[:, 128 * t : 128 * t + 128] = total[64 + 8 * t : 72 + 8 * t]
    proj_ref[...] = total[88:96]
    for t in range(6):
        width = min(128, TABLE - 128 * t)
        bias_ref[:, 128 * t : 128 * t + width] = total[96 + 8 * t : 104 + 8 * t, :width]
    merge_gain_ref[...] = total[144:160]
    norm_gain_ref[...] = total[160:164]


def unpack(got):
    shapes = [(8, 384), (8, 128), (32, 256), (4, 128), (16, 128), (8, TABLE)]
    return pl.pallas_call(
        unpack_kernel,
        out_shape=[jax.ShapeDtypeStruct(s, F32) for s in shapes],
        in_specs=vmem(1),
        out_specs=vmem(6),
        compiler_params=PARAMS,
    )(got)


def swapped(value, axis, bit):
    count = lax.axis_size(axis)
    return lax.ppermute(value, axis, [(i ^ bit, i) for i in range(count)])


def diagonal(block, distance):
    route = [(((i // 4 - distance) % 64) * 4 + (i % 4 - distance) % 4, i) for i in range(256)]
    return lax.ppermute(block, AXES, route)


def spread_over(parts, axes):
    return lax.all_to_all(parts, axes, 0, 0, tiled=True)


def quarters(corner, north, east, stay):
    top = jnp.concatenate([corner, north], axis=1)
    return jnp.concatenate([top, jnp.concatenate([east, stay], axis=1)], axis=0)


def on_device(features, norm_gain, qkv_weight, proj_weight, bias_table, merge_gain, merge_weight, merged_cot):
    last = (lax.axis_index(LAT) == total_of(LAT) - 1).astype(jnp.int32).reshape(1)
    gain, wide_gain = norm_gain.reshape(1, 512), merge_gain.reshape(1, 2048)
    own = features.transpose(1, 2, 0, 3).reshape(6, 48, 512)
    own, merged_cot = lax.optimization_barrier((own, merged_cot))
    cot = merged_cot.transpose(1, 2, 0, 3).reshape(3, 24, 1024)
    west = moved(own[:, :24], LON, -1)
    south = moved(own[:3, 24:], LAT, -1)
    corner = diagonal(own[:3, :24], -1)
    cot_west = moved(cot[1:, :12], LON, -1)
    cot_south = moved(cot[:2, 12:], LAT, -1)
    cot_corner = diagonal(cot[:2, :12], -1)
    bias, mask = bias_of(bias_table, last)
    flat = own.reshape(TOK, 512)
    flat, bias, mask, west, south, corner = lax.optimization_barrier((flat, bias, mask, west, south, corner))
    x, qkv, p, rows, block, first, final = attend(
        flat, west.reshape(144, 512), south.reshape(72, 512), corner.reshape(72, 512),
        gain, qkv_weight, proj_weight, bias, mask,
    )
    following = moved(first, LAT, -1)
    prev = moved(final, LAT, 1)
    core = lax.axis_index("c").astype(jnp.int32).reshape(1)
    pair, hats, scale, all_cot = stack(block, prev, following, cot, cot_west, cot_south, cot_corner, wide_gain)
    early = spread_over(pair, CLOSE)
    attn_cot, merge_gain_part = merge(hats, scale, all_cot, wide_gain, merge_weight)
    rows_theirs = swapped(rows, "c", 1)
    home, norm_gain_part, columns, columns_out, left, right = attend_back(
        core, attn_cot, x, qkv, p, qkv_weight, proj_weight, gain
    )
    columns_theirs = swapped(columns_out, "c", 1)
    small = small_grads(left, right, merge_gain_part, norm_gain_part)
    columns_theirs, small = lax.optimization_barrier((columns_theirs, small))
    late = late_grads(rows, rows_theirs, columns, columns_theirs, small, swapped(small, "c", 1))
    late, early, home = lax.optimization_barrier((late, early, home))
    late = spread_over(late, NEAR)
    stay, merged, north, east, corner = home_parts(hats, wide_gain, merge_weight, home)
    north, east, corner = moved(north, LAT, 1), moved(east, LON, 1), diagonal(corner, 1)
    last = fold(pair_grad(early), late)
    last, north, east, corner = lax.optimization_barrier((last, north, east, corner))
    got = spread_over(last, FAR)
    grad = quarters(
        corner[32:].reshape(3, 24, 512), north[32:].reshape(3, 24, 512), east[64:].reshape(3, 24, 512),
        stay.reshape(3, 24, 512),
    )

    def wide(left, right, rows):
        return jnp.concatenate([left, right], axis=1).reshape(rows, 12, 1024)

    coarse = quarters(
        wide(corner[:12], corner[16:28], 1), wide(north[:12], north[16:28], 1),
        wide(east[:24], east[32:56], 2), merged[:24].reshape(2, 12, 1024),
    )
    merged = coarse.reshape(3, 6, 4, 1024).transpose(2, 0, 1, 3)
    features_grad = grad.reshape(6, 12, 4, 512).transpose(2, 0, 1, 3)
    qkv_grad, proj_grad, merge_grad, norm_gain_grad, merge_gain_grad, bias_grad = unpack(got)
    return (
        merged,
        features_grad,
        qkv_grad,
        proj_grad,
        merge_grad,
        norm_gain_grad.reshape(-1),
        merge_gain_grad.reshape(-1),
        bias_grad,
    )


def solution(mesh):
    fine = Mesh(mesh.devices.reshape(4, 2, 8, 2, 2), AXES)
    field = P(None, LAT, LON, None)
    return jax.shard_map(
        on_device,
        mesh=fine,
        in_specs=(field, P(), P(), P(), P(), P(), P(), field),
        out_specs=(field, field, P(LON, LAT), P(LON, LAT), P(LON, LAT), P(), P(), P()),
        check_vma=False,
    )
```
